128 devices in a mesh: cam: 4 (over x_hi, core), frame: 32 (over z, y, x_lo).
Axes of the slice: x: 4 (x_hi: 2, x_lo: 2; x = x_hi * 2 + x_lo), y: 4, z: 4, core: 2. Of those that a mesh axis runs over, the one named last changes fastest.
Arguments:
- hidden: bfloat16 [4, 32, 512, 2048], P('cam', 'frame'), may hold values from -6 to 6
- t_query: bfloat16 [4, 32, 512, 1024], P('cam', 'frame'), may hold values from -16 to 16
- t_key: bfloat16 [4, 32, 512, 1024], P('cam', 'frame'), may hold values from -6 to 6
- t_value: bfloat16 [4, 32, 512, 1024], P('cam', 'frame'), may hold values from -6 to 6
- frame_offsets: int32 [32], replicated, may hold values from 0 to 63, as said below
- cycle_sides: int32 [4, 2], P('cam'), may hold values from 0 to 3, as said below
- w_temporal_out: bfloat16 [1024, 2048], replicated, may hold values from -0.1875 to 0.1875
- norm_gain: bfloat16 [2048], replicated, may hold values from 0.099609375 to 1.8984375
- w_query: bfloat16 [2048, 1024], replicated, may hold values from -0.25 to 0.25
- w_key: bfloat16 [2048, 1024], replicated, may hold values from -0.25 to 0.25
- w_value: bfloat16 [2048, 1024], replicated, may hold values from -0.125 to 0.125
- w_cross_out: bfloat16 [1024, 2048], replicated, may hold values from -0.1875 to 0.1875
- side_embed: bfloat16 [2, 1024], replicated, may hold values from -4 to 4
Outputs:
- mixed: bfloat16 [4, 32, 512, 2048], P('cam', 'frame')
The draws below stay inside these ranges and needn't reach their ends.
Inputs may be any that keep to these rules, and one draw needn't show every extreme that they name: `frame_offsets`: offset of frame f is 2 f or 2 f + 1; the last frame's is 63. `cycle_sides`: row c holds (c - 1) mod 4 and (c + 1) mod 4 in either order.
All inputs are finite; a program needn't handle non-finite values.
Results may differ from the reference program's by a relative error of at most 0.03.
Values may be sent and summed in bfloat16 or wider, within the bound.
No kernel may reach another device: no remote copies, remote signals or barrier semaphores. Data moves between devices by JAX's collectives and lax.ppermute only.
A program may use at most 256 MiB of HBM per device.

```python
import math
import jax
import jax.numpy as jnp
from jax import lax

D = 2048
HEADS = 8
HEAD_DIM = 128
POS = 512
INNER = 1024
CAMS = 4
FRAMES = 32


def projection_draw(key):
    base = jnp.clip(jax.random.normal(key, (D, INNER), jnp.float32), -6.0, 6.0) * (1.0 / D) ** 0.5
    return jnp.clip(base, -0.25, 0.25).astype(jnp.bfloat16)


def draw_t_query(key, part):
    key = jax.random.fold_in(key, 3)
    return jnp.clip(jax.random.normal(key, (CAMS, FRAMES, POS, INNER), jnp.float32), -6.0, 6.0).astype(jnp.bfloat16)


def draw_t_key(key, part):
    key = jax.random.fold_in(key, 5)
    return jnp.clip(jax.random.normal(key, (CAMS, FRAMES, POS, INNER), jnp.float32), -6.0, 6.0).astype(jnp.bfloat16)


def draw_frame_offsets(key, part):
    key = jax.random.fold_in(key, 7)
    extra = jax.random.randint(key, (FRAMES,), 0, 2)
    steps_i = jnp.arange(FRAMES, dtype=jnp.int32)
    extra = jnp.where(steps_i == 0, 0, extra)
    extra = jnp.where(steps_i == FRAMES - 1, 1, extra)
    return (2 * steps_i + extra).astype(jnp.int32)


def draw_cycle_sides(key, part):
    key = jax.random.fold_in(key, 9)
    flip = jax.random.randint(key, (CAMS,), 0, 2)
    camera = jnp.arange(CAMS, dtype=jnp.int32)
    lower = (camera + CAMS - 1) % CAMS
    upper = (camera + 1) % CAMS
    first = jnp.where(flip == 1, upper, lower)
    second = jnp.where(flip == 1, lower, upper)
    return jnp.stack([first, second], axis=1).astype(jnp.int32)


def draw_w_query(key, part):
    key = jax.random.fold_in(key, 11)
    return projection_draw(key)


def draw_w_key(key, part):
    key = jax.random.fold_in(key, 17)
    return projection_draw(key)


def steps_of(rng, dims, shards, least, largest):
    def one(axis_at, parts):
        steps = jax.random.uniform(jax.random.fold_in(jax.random.fold_in(rng, 6), axis_at), (parts,), jnp.float32, least / len(shards), largest / len(shards))
        return jnp.repeat(jnp.exp(steps), dims[axis_at] // parts).reshape((-1,) + (1,) * (len(dims) - axis_at - 1))

    level = one(*shards[0])
    for cut in shards[1:]:
        level = level * one(*cut)
    return level


def bell_draw(own_key, dims, width, limit, cuts=(), kind=jnp.bfloat16):
    gain = steps_of(own_key, dims, cuts, -0.22, 0.18) if cuts else 1.0
    values = jax.random.normal(own_key, dims, jnp.float32) * width * gain
    return jnp.minimum(jnp.maximum(values, -limit), limit).astype(kind)


def setup_inputs(seed: int = 0) -> dict:
    keys = jax.random.split(jax.random.key(seed), 14)
    hidden = bell_draw(keys[0], (CAMS, FRAMES, POS, D), 1.0, 6.0, ((0, 4), (1, 32)))
    t_query = draw_t_query(jax.random.fold_in(keys[13], 71), 0)
    t_key = draw_t_key(jax.random.fold_in(keys[13], 71), 0)
    t_value = bell_draw(keys[3], (CAMS, FRAMES, POS, INNER), 1.0, 6.0, ((0, 4), (1, 32)))
    frame_offsets = draw_frame_offsets(jax.random.fold_in(keys[13], 71), 0)
    cycle_sides = draw_cycle_sides(jax.random.fold_in(keys[13], 71), 0)
    w_temporal_out = bell_draw(keys[6], (INNER, D), INNER ** -0.5, 0.1875)
    norm_gain = jnp.clip(1.0 + 0.18 * jax.random.normal(keys[7], (D,), jnp.float32), 0.099609375, 1.8984375).astype(jnp.bfloat16)
    w_query = draw_w_query(jax.random.fold_in(keys[13], 71), 0)
    w_key = draw_w_key(jax.random.fold_in(keys[13], 71), 0)
    w_value = bell_draw(keys[10], (D, INNER), D ** -0.5, 0.125)
    w_cross_out = bell_draw(keys[11], (INNER, D), INNER ** -0.5, 0.1875)
    side_embed = bell_draw(keys[12], (2, INNER), 1.0, 4.0)
    return {"hidden": hidden, "t_query": t_query, "t_key": t_key, "t_value": t_value, "frame_offsets": frame_offsets, "cycle_sides": cycle_sides, "w_temporal_out": w_temporal_out, "norm_gain": norm_gain, "w_query": w_query, "w_key": w_key, "w_value": w_value, "w_cross_out": w_cross_out, "side_embed": side_embed}


def rotary_angles(offsets):
    half_dim = HEAD_DIM // 2
    steps_f = jnp.arange(half_dim).astype(jnp.float32)
    frequencies = 10000.0 ** (-steps_f / half_dim)
    return offsets.astype(jnp.float32)[..., None] * frequencies

def rotate_pairs(values_in, angles):
    half_dim = values_in.shape[-1] // 2
    cosine = jnp.cos(angles)
    sine = jnp.sin(angles)
    first = values_in[..., :half_dim]
    second = values_in[..., half_dim:]
    return jnp.concatenate([first * cosine - second * sine, first * sine + second * cosine], axis=-1)

def softmax_rows(scores):
    top_val = lax.optimization_barrier(jnp.max(scores, axis=-1, keepdims=True))
    expo = jnp.exp(scores - top_val)
    return expo / lax.optimization_barrier(jnp.sum(expo, axis=-1, keepdims=True))

def reference(hidden, t_query, t_key, t_value, frame_offsets, cycle_sides, w_temporal_out, norm_gain, w_query, w_key, w_value, w_cross_out, side_embed):
    score_scale = 1.0 / math.sqrt(HEAD_DIM)
    shape5 = (CAMS, FRAMES, POS, HEADS, HEAD_DIM)
    angles = rotary_angles(frame_offsets)[None, :, None, None, :]
    queries = rotate_pairs(t_query.reshape(shape5).astype(jnp.float32), angles).astype(jnp.bfloat16)
    keys_rot = rotate_pairs(t_key.reshape(shape5).astype(jnp.float32), angles).astype(jnp.bfloat16)
    values_t = t_value.reshape(shape5)
    scores = jnp.einsum('cfphd,cgphd->cphfg', queries.astype(jnp.float32), keys_rot.astype(jnp.float32)) * score_scale
    weights_t = softmax_rows(scores).astype(jnp.bfloat16)
    temporal = jnp.einsum('cphfg,cgphd->cfphd', weights_t.astype(jnp.float32), values_t.astype(jnp.float32)).astype(jnp.bfloat16)
    temporal_proj = jnp.dot(temporal.reshape(-1, INNER), w_temporal_out, preferred_element_type=jnp.float32)
    stream = (hidden.reshape(-1, D).astype(jnp.float32) + temporal_proj).astype(jnp.bfloat16)
    stream_f = stream.astype(jnp.float32)
    normed = (stream_f * lax.rsqrt(lax.optimization_barrier(jnp.mean(stream_f * stream_f, axis=-1, keepdims=True)) + 1e-06) * norm_gain.astype(jnp.float32)).astype(jnp.bfloat16)
    cross_q = jnp.dot(normed, w_query, preferred_element_type=jnp.float32).astype(jnp.bfloat16).reshape(CAMS, FRAMES, POS, INNER)
    cross_k = jnp.dot(normed, w_key, preferred_element_type=jnp.float32).astype(jnp.bfloat16).reshape(CAMS, FRAMES, POS, INNER)
    cross_v = jnp.dot(normed, w_value, preferred_element_type=jnp.float32).astype(jnp.bfloat16).reshape(CAMS, FRAMES, POS, INNER)
    side_f = side_embed.astype(jnp.float32)

    def one_view(index):
        camera = index // FRAMES
        frame_at = index % FRAMES
        left_cam = cycle_sides[camera, 0]
        right_cam = cycle_sides[camera, 1]
        left_key = (cross_k[left_cam, frame_at].astype(jnp.float32) + side_f[0]).astype(jnp.bfloat16)
        right_key = (cross_k[right_cam, frame_at].astype(jnp.float32) + side_f[1]).astype(jnp.bfloat16)
        keys_all = jnp.concatenate([cross_k[camera, frame_at], left_key, right_key], axis=0).reshape(3 * POS, HEADS, HEAD_DIM)
        vals_all = jnp.concatenate([cross_v[camera, frame_at], cross_v[left_cam, frame_at], cross_v[right_cam, frame_at]], axis=0).reshape(3 * POS, HEADS, HEAD_DIM)
        query_rows = cross_q[camera, frame_at].reshape(POS, HEADS, HEAD_DIM)
        scores_c = jnp.einsum('qhd,khd->hqk', query_rows.astype(jnp.float32), keys_all.astype(jnp.float32)) * score_scale
        weights_c = softmax_rows(scores_c).astype(jnp.bfloat16)
        result = jnp.einsum('hqk,khd->qhd', weights_c.astype(jnp.float32), vals_all.astype(jnp.float32))
        return result.astype(jnp.bfloat16).reshape(POS, INNER)
    cross = lax.map(one_view, jnp.arange(CAMS * FRAMES, dtype=jnp.int32))
    cross_proj = jnp.dot(cross.reshape(-1, INNER), w_cross_out, preferred_element_type=jnp.float32)
    mixed = (stream.astype(jnp.float32) + cross_proj).astype(jnp.bfloat16)
    return mixed.reshape(CAMS, FRAMES, POS, D)
```

```python
import functools
import math

import jax
import jax.numpy as jnp
from jax import lax
from jax.experimental import pallas as pl
from jax.experimental.pallas import tpu as pltpu
from jax.sharding import PartitionSpec as P

HEADS = 8
HEAD_DIM = 128
MIB = 1 << 20
VMEM_LIMIT = 60 * MIB
F32 = jnp.float32
BF16 = jnp.bfloat16
EXP2_SCALE = math.log2(math.e) / math.sqrt(HEAD_DIM)


def dot_f32(a, b):
    return jnp.dot(a, b, preferred_element_type=F32)


def dot_nt(a, b):
    return lax.dot_general(a, b, (((1,), (1,)), ((), ())), preferred_element_type=F32)


def rotary_angles(offsets):
    half_dim = HEAD_DIM // 2
    steps_f = jnp.arange(half_dim).astype(F32)
    frequencies = 10000.0 ** (-steps_f / half_dim)
    return offsets.astype(F32)[..., None] * frequencies


def temporal_kernel(group, heads_at_once, *refs):
    q_ref, k_ref, v_ref, cos_ref, sin_ref = refs[:5]
    o_ref = refs[-1]
    rows = q_ref.shape[0]
    cosine = cos_ref[...]
    sine = sin_ref[...]
    row_at = lax.broadcasted_iota(jnp.int32, (rows, rows), 0)
    key_at = lax.broadcasted_iota(jnp.int32, (rows, rows), 1)
    same = lax.rem(row_at, group) == lax.rem(key_at, group)

    def rotated(part):
        part = part.astype(F32)
        return (part * cosine + pltpu.roll(part, HEAD_DIM // 2, 1) * sine).astype(BF16)

    for head in range(heads_at_once):
        at = slice(head * HEAD_DIM, (head + 1) * HEAD_DIM)
        scores = dot_nt(rotated(q_ref[:, at]), rotated(k_ref[:, at]))
        scores = jnp.where(same, scores, -jnp.inf)
        top = jnp.max(scores, axis=-1, keepdims=True)
        expo = jnp.exp2((scores - top) * EXP2_SCALE)
        weights = (expo * (1.0 / jnp.sum(expo, axis=-1, keepdims=True))).astype(BF16)
        o_ref[:, at] = dot_f32(weights, v_ref[:, at]).astype(BF16)


def temporal(packed, cosine, sine, group, into):
    rows = packed.shape[0]
    at_once = 2
    width = at_once * HEAD_DIM
    steps = HEADS // at_once
    in_specs = [
        pl.BlockSpec((rows, width), lambda i: (0, i)),
        pl.BlockSpec((rows, width), lambda i: (0, steps + i)),
        pl.BlockSpec((rows, width), lambda i: (0, 2 * steps + i)),
        pl.BlockSpec((rows, HEAD_DIM), lambda i: (0, 0)),
        pl.BlockSpec((rows, HEAD_DIM), lambda i: (0, 0)),
    ]
    args = [packed, packed, packed, cosine, sine]
    aliases = {}
    first = 0
    out_width = HEADS * HEAD_DIM
    if into is not None:
        in_specs.append(pl.BlockSpec(memory_space=pl.ANY))
        args.append(into)
        aliases = {5: 0}
        first = 3 * steps
        out_width = into.shape[1]
    return pl.pallas_call(
        functools.partial(temporal_kernel, group, at_once),
        grid=(steps,),
        in_specs=in_specs,
        out_specs=pl.BlockSpec((rows, width), lambda i: (0, first + i)),
        out_shape=jax.ShapeDtypeStruct((rows, out_width), BF16),
        input_output_aliases=aliases,
        compiler_params=pltpu.CompilerParams(vmem_limit_bytes=VMEM_LIMIT),
        cost_estimate=pl.CostEstimate(
            flops=4 * rows * rows * HEADS * HEAD_DIM,
            bytes_accessed=8 * rows * HEADS * HEAD_DIM,
            transcendentals=rows * rows * HEADS,
        ),
        name="temporal",
    )(*args)


def project_kernel(*refs):
    t_ref, hidden_ref, w_out_ref, gain_ref, w_key_ref, w_value_ref = refs[:6]
    stream_ref, normed_ref, kv_ref = refs[-3:]
    step = pl.program_id(0)

    @pl.when(step < 2)
    def _():
        cols = pl.ds(pl.multiple_of(step * 1024, 1024), 1024)
        part = dot_f32(t_ref[...], w_out_ref[...])
        stream_ref[:, cols] = (hidden_ref[:, cols].astype(F32) + part).astype(BF16)

    @pl.when(step == 2)
    def _():
        stream = stream_ref[...].astype(F32)
        scale = lax.rsqrt(jnp.mean(stream * stream, axis=-1, keepdims=True) + 1e-06)
        normed_ref[...] = (stream * scale * gain_ref[...].astype(F32)).astype(BF16)

    @pl.when((step >= 2) & (step < 4))
    def _():
        kv_ref[...] = dot_f32(normed_ref[...], w_key_ref[...]).astype(BF16)

    @pl.when(step >= 4)
    def _():
        kv_ref[...] = dot_f32(normed_ref[...], w_value_ref[...]).astype(BF16)


def project(t_out, t_block, hidden, w_out, gain, w_key, w_value, chunk, into):
    rows = t_out.shape[0]
    inner = HEADS * HEAD_DIM
    width = hidden.shape[1]
    in_specs = [
        pl.BlockSpec((rows, inner), lambda i: (0, t_block)),
        pl.BlockSpec((rows, width), lambda i: (chunk, 0)),
        pl.BlockSpec((inner, 1024), lambda i: (0, jnp.minimum(i, 1))),
        pl.BlockSpec((1, width), lambda i: (0, 0)),
        pl.BlockSpec((width, 512), lambda i: (0, jnp.clip(i - 2, 0, 1))),
        pl.BlockSpec((width, 512), lambda i: (0, jnp.clip(i - 4, 0, 1))),
    ]
    args = [t_out, hidden, w_out, gain, w_key, w_value]
    aliases = {}
    if into is not None:
        in_specs += [pl.BlockSpec(memory_space=pl.ANY)] * 2
        args += list(into)
        aliases = {6: 0, 7: 1}
    return pl.pallas_call(
        project_kernel,
        grid=(6,),
        in_specs=in_specs,
        out_specs=[
            pl.BlockSpec((rows, width), lambda i: (chunk, 0)),
            pl.BlockSpec((rows, width), lambda i: (chunk, 0)),
            pl.BlockSpec((rows, 512), lambda i: (0, jnp.clip(i - 2, 0, 3))),
        ],
        out_shape=[
            jax.ShapeDtypeStruct(hidden.shape, BF16),
            jax.ShapeDtypeStruct(hidden.shape, BF16),
            jax.ShapeDtypeStruct((rows, 2 * inner), BF16),
        ],
        input_output_aliases=aliases,
        compiler_params=pltpu.CompilerParams(vmem_limit_bytes=VMEM_LIMIT),
        cost_estimate=pl.CostEstimate(
            flops=6 * rows * inner * width,
            bytes_accessed=16 * MIB,
            transcendentals=0,
        ),
        name="project",
    )(*args)


def first_kernel(sides, heads_at_once, *refs):
    normed_ref, w_query_ref, embed_ref = refs[:3]
    count = len(sides)
    key_refs = refs[3 : 3 + count]
    value_refs = refs[3 + count : 3 + 2 * count]
    q_ref, acc_ref, top_ref, total_ref = refs[3 + 2 * count :]
    step = pl.program_id(0)
    lane = lax.broadcasted_iota(jnp.int32, (256, HEAD_DIM), 1)
    for block in range(2):
        rows = slice(block * 256, (block + 1) * 256)
        q_ref[rows, :] = dot_f32(normed_ref[rows, :], w_query_ref[...]).astype(BF16)
    for head in range(heads_at_once):
        at = slice(head * HEAD_DIM, (head + 1) * HEAD_DIM)
        keys = []
        for side, key_ref in zip(sides, key_refs):
            key = key_ref[:, at]
            if side is not None:
                key = (key.astype(F32) + embed_ref[side : side + 1, at]).astype(BF16)
            keys.append(key)
        for block in range(2):
            rows = slice(block * 256, (block + 1) * 256)
            query = q_ref[rows, at]
            scores = [dot_nt(query, key) for key in keys]
            top = functools.reduce(jnp.maximum, scores)
            top = jnp.max(top, axis=-1, keepdims=True)
            total = 0.0
            acc = 0.0
            for score, value_ref in zip(scores, value_refs):
                expo = jnp.exp2((score - top) * EXP2_SCALE)
                total = total + jnp.sum(expo, axis=-1, keepdims=True)
                acc = acc + dot_f32(expo.astype(BF16), value_ref[:, at])
            acc_ref[rows, at] = acc
            mine = lane == step * heads_at_once + head
            top_ref[rows, :] = jnp.where(mine, top, top_ref[rows, :])
            total_ref[rows, :] = jnp.where(mine, total, total_ref[rows, :])


def first_part(normed, w_query, embeds, views, sides):
    rows, width = normed.shape
    inner = HEADS * HEAD_DIM
    at_once = 2
    cols = at_once * HEAD_DIM
    steps = HEADS // at_once
    key_spec = pl.BlockSpec((views[0].shape[0], cols), lambda i: (0, i))
    value_spec = pl.BlockSpec((views[0].shape[0], cols), lambda i: (0, steps + i))
    return pl.pallas_call(
        functools.partial(first_kernel, sides, at_once),
        grid=(steps,),
        in_specs=[
            pl.BlockSpec((rows, width), lambda i: (0, 0)),
            pl.BlockSpec((width, cols), lambda i: (0, i)),
            pl.BlockSpec((2, cols), lambda i: (0, i)),
        ]
        + [key_spec] * len(views)
        + [value_spec] * len(views),
        out_specs=[
            pl.BlockSpec((rows, cols), lambda i: (0, i)),
            pl.BlockSpec((rows, cols), lambda i: (0, i)),
            pl.BlockSpec((rows, HEAD_DIM), lambda i: (0, 0)),
            pl.BlockSpec((rows, HEAD_DIM), lambda i: (0, 0)),
        ],
        out_shape=[
            jax.ShapeDtypeStruct((rows, inner), BF16),
            jax.ShapeDtypeStruct((rows, inner), F32),
            jax.ShapeDtypeStruct((rows, HEAD_DIM), F32),
            jax.ShapeDtypeStruct((rows, HEAD_DIM), F32),
        ],
        compiler_params=pltpu.CompilerParams(vmem_limit_bytes=VMEM_LIMIT),
        cost_estimate=pl.CostEstimate(
            flops=2 * rows * width * inner + 4 * rows * 256 * len(views) * inner,
            bytes_accessed=14 * MIB,
            transcendentals=rows * 256 * len(views) * HEADS,
        ),
        name="first_part",
    )(normed, w_query, embeds, *views, *views)


def last_kernel(
    q_ref, acc_ref, top_ref, total_ref, kv_ref, embed_ref, stream_ref, w_hbm, o_ref, w_ref, out_ref, sem
):
    step = pl.program_id(0)
    inner = HEADS * HEAD_DIM
    fetch = pltpu.make_async_copy(w_hbm, w_ref, sem)

    @pl.when(step == 0)
    def _():
        fetch.start()

    for head in range(HEADS):
        at = slice(head * HEAD_DIM, (head + 1) * HEAD_DIM)
        value_at = slice(inner + head * HEAD_DIM, inner + (head + 1) * HEAD_DIM)
        key = (kv_ref[:, at].astype(F32) + embed_ref[1:2, at]).astype(BF16)
        scores = dot_nt(q_ref[:, at], key)
        top_before = top_ref[:, head : head + 1]
        top = jnp.maximum(top_before, jnp.max(scores, axis=-1, keepdims=True))
        keep = jnp.exp2((top_before - top) * EXP2_SCALE)
        expo = jnp.exp2((scores - top) * EXP2_SCALE)
        total = total_ref[:, head : head + 1] * keep + jnp.sum(expo, axis=-1, keepdims=True)
        acc = acc_ref[:, at] * keep + dot_f32(expo.astype(BF16), kv_ref[:, value_at])
        out_ref[:, at] = (acc * (1.0 / total)).astype(BF16)

    @pl.when(step == 0)
    def _():
        fetch.wait()

    for part in range(4):
        cols = slice(part * 512, (part + 1) * 512)
        product = dot_f32(out_ref[...], w_ref[:, cols])
        o_ref[:, cols] = (stream_ref[:, cols].astype(F32) + product).astype(BF16)


def last_part(query, acc, top, total, view, embeds, stream, w_out):
    rows, width = stream.shape
    inner = HEADS * HEAD_DIM
    block = 256
    return pl.pallas_call(
        last_kernel,
        grid=(rows // block,),
        in_specs=[
            pl.BlockSpec((block, inner), lambda i: (i, 0)),
            pl.BlockSpec((block, inner), lambda i: (i, 0)),
            pl.BlockSpec((block, HEAD_DIM), lambda i: (i, 0)),
            pl.BlockSpec((block, HEAD_DIM), lambda i: (i, 0)),
            pl.BlockSpec(view.shape, lambda i: (0, 0)),
            pl.BlockSpec(embeds.shape, lambda i: (0, 0)),
            pl.BlockSpec((block, width), lambda i: (i, 0)),
            pl.BlockSpec(memory_space=pl.ANY),
        ],
        out_specs=pl.BlockSpec((block, width), lambda i: (i, 0)),
        out_shape=jax.ShapeDtypeStruct((rows, width), BF16),
        scratch_shapes=[
            pltpu.VMEM(w_out.shape, BF16),
            pltpu.VMEM((block, inner), BF16),
            pltpu.SemaphoreType.DMA,
        ],
        compiler_params=pltpu.CompilerParams(vmem_limit_bytes=VMEM_LIMIT),
        cost_estimate=pl.CostEstimate(
            flops=2 * rows * width * inner + 4 * rows * view.shape[0] * inner,
            bytes_accessed=12 * MIB,
            transcendentals=rows * view.shape[0] * HEADS,
        ),
        name="last_part",
    )(query, acc, top, total, view, embeds, stream, w_out)


def shards(
    hidden,
    t_query,
    t_key,
    t_value,
    frame_offsets,
    cycle_sides,
    w_temporal_out,
    norm_gain,
    w_query,
    w_key,
    w_value,
    w_cross_out,
    side_embed,
):
    rows_here = hidden.shape[2]
    model_width = hidden.shape[3]
    inner = t_query.shape[3]
    frames = lax.axis_size("frame")
    half = rows_here // 2
    group = half // frames
    hidden = hidden.reshape(rows_here, model_width)
    t_query = t_query.reshape(rows_here, inner)
    t_key = t_key.reshape(rows_here, inner)
    t_value = t_value.reshape(rows_here, inner)
    gain = norm_gain.reshape(1, model_width)

    angles = rotary_angles(frame_offsets)
    cosine = jnp.cos(angles)
    sine = jnp.sin(angles)
    cosine = jnp.repeat(jnp.concatenate([cosine, cosine], axis=-1), group, axis=0)
    sine = jnp.repeat(jnp.concatenate([-sine, sine], axis=-1), group, axis=0)

    def exchange(value):
        return lax.all_to_all(value, "frame", split_axis=0, concat_axis=0, tiled=True)

    def to_near(value):
        return lax.ppermute(value, "cam", [(0, 1), (1, 0), (2, 3), (3, 2)])

    def to_far(value):
        return lax.ppermute(value, "cam", [(0, 3), (3, 0), (1, 2), (2, 1)])

    near_cam = lax.axis_index("cam") ^ 1
    near_left = cycle_sides[0, 0] == near_cam
    side_f = side_embed.astype(F32)
    embeds = jnp.where(near_left, side_f, side_f[::-1])

    packed_a = jnp.concatenate([t_query[:half], t_key[:half], t_value[:half]], axis=1)
    packed_b = jnp.concatenate(
        [t_query[half:], t_key[half:], t_value[half:], jnp.zeros((half, inner), BF16)], axis=1
    )
    got_a = exchange(packed_a)
    packed_b = temporal(got_a, cosine, sine, group, packed_b)
    got_b = exchange(packed_b)
    out_b = temporal(got_b, cosine, sine, group, None)
    back_b = exchange(out_b)

    weights = (w_temporal_out, gain, w_key, w_value)
    stream, normed, kv_a = project(got_b, 3, hidden, *weights, 0, None)
    far_a = to_far(kv_a)
    near_a = to_near(kv_a)
    stream, normed, kv_b = project(back_b, 0, hidden, *weights, 1, (stream, normed))
    far_b = to_far(kv_b)
    near_b = to_near(kv_b)
    query, acc, top, total = first_part(
        normed, w_query, embeds, [kv_a, kv_b, near_a, near_b, far_a], (None, None, 0, 0, 1)
    )
    mixed = last_part(query, acc, top, total, far_b, embeds, stream, w_cross_out)
    return mixed.reshape(1, 1, rows_here, model_width)


def solution(mesh):
    in_specs = (
        P("cam", "frame", None, None),
        P("cam", "frame", None, None),
        P("cam", "frame", None, None),
        P("cam", "frame", None, None),
        P(),
        P("cam", None),
        P(),
        P(),
        P(),
        P(),
        P(),
        P(),
        P(),
    )
    out_specs = P("cam", "frame", None, None)
    return jax.shard_map(shards, mesh=mesh, in_specs=in_specs, out_specs=out_specs, check_vma=False)
```

```python
import functools
import math

import jax
import jax.numpy as jnp
from jax import lax
from jax.experimental import pallas as pl
from jax.experimental.pallas import tpu as pltpu
from jax.sharding import PartitionSpec as P

HEADS = 8
HEAD_DIM = 128
MIB = 1 << 20
F32 = jnp.float32
BF16 = jnp.bfloat16
EXP2_SCALE = math.log2(math.e) / math.sqrt(HEAD_DIM)


def dot_f32(a, b):
    return jnp.dot(a, b, preferred_element_type=F32)


def dot_nt(a, b):
    return lax.dot_general(a, b, (((1,), (1,)), ((), ())), preferred_element_type=F32)


def rotary_frequencies():
    half_dim = HEAD_DIM // 2
    steps_f = jnp.arange(half_dim).astype(F32)
    frequencies = 10000.0 ** (-steps_f / half_dim)
    return jnp.concatenate([frequencies, frequencies])[None, :]


VMEM = pl.BlockSpec(memory_space=pltpu.VMEM)
HBM = pl.BlockSpec(memory_space=pltpu.HBM)


def columns(head):
    return slice(head * HEAD_DIM, (head + 1) * HEAD_DIM)


def with_ones(values):
    return jnp.concatenate([values, jnp.ones_like(values)], axis=1)


def copy_all(pairs, sems):
    copies = [pltpu.make_async_copy(a, b, sems.at[i]) for i, (a, b) in enumerate(pairs)]
    for copy in copies:
        copy.start()
    for copy in copies:
        copy.wait()


def in_hbm(*arrays):
    return [pltpu.with_memory_space_constraint(array, pltpu.HBM) for array in arrays]


def pack_kernel(q_ref, k_ref, v_ref, offset_ref, frequency_ref, o_ref, cos_ref, sin_ref, sems):
    rows, inner = o_ref.shape[0], q_ref.shape[1]
    moves = [
        pltpu.make_async_copy(ref.at[:rows, :], o_ref.at[:, i * inner : (i + 1) * inner], sems.at[i])
        for i, ref in enumerate((q_ref, k_ref, v_ref))
    ]
    for move in moves:
        move.start()
    frames = offset_ref.shape[0]
    group = rows // frames
    angles = offset_ref[...] * frequency_ref[...]
    lane = lax.broadcasted_iota(jnp.int32, angles.shape, 1)
    cosine = jnp.cos(angles)
    sine = jnp.sin(angles)
    sine = jnp.where(lane < HEAD_DIM // 2, -sine, sine)
    for frame in range(frames):
        at = slice(frame * group, (frame + 1) * group)
        cos_ref[at, :] = jnp.broadcast_to(cosine[frame : frame + 1, :], (group, HEAD_DIM))
        sin_ref[at, :] = jnp.broadcast_to(sine[frame : frame + 1, :], (group, HEAD_DIM))
    for move in moves:
        move.wait()


def pack(query, key, value, offsets, frequencies):
    rows, inner = query.shape
    half = rows // 2
    table = pltpu.VMEM((half, HEAD_DIM), F32)
    return pl.pallas_call(
        pack_kernel,
        in_specs=[HBM] * 3 + [VMEM] * 2,
        out_specs=[VMEM] * 3,
        out_shape=[pltpu.VMEM((half, 3 * inner), BF16), table, table],
        scratch_shapes=[pltpu.SemaphoreType.DMA((3,))],
        compiler_params=pltpu.CompilerParams(vmem_limit_bytes=4 * MIB),
        cost_estimate=pl.CostEstimate(flops=0, bytes_accessed=6 * rows * inner, transcendentals=0),
        name="pack",
    )(*in_hbm(query, key, value), offsets, frequencies)


def temporal_kernel(group, packed_ref, cos_ref, sin_ref, *refs):
    rows = packed_ref.shape[0]
    inner = HEADS * HEAD_DIM
    count = max(len(refs) - 2, 0)
    first = 0
    o_ref = refs[count]
    copies = []
    if count:
        first = count * inner
        for i, ref in enumerate(refs[:count]):
            to = o_ref.at[:, i * inner : (i + 1) * inner]
            copies.append(pltpu.make_async_copy(ref.at[rows:, :], to, refs[count + 1].at[i]))
            copies[-1].start()
    cosine = cos_ref[...]
    sine = sin_ref[...]
    row_at = lax.broadcasted_iota(jnp.int32, (rows, rows), 0)
    key_at = lax.broadcasted_iota(jnp.int32, (rows, rows), 1)
    same = lax.rem(row_at, group) == lax.rem(key_at, group)
    def rotated(part):
        part = part.astype(F32)
        return (part * cosine + pltpu.roll(part, HEAD_DIM // 2, 1) * sine).astype(BF16)

    for head in range(HEADS):
        query = rotated(packed_ref[:, columns(head)])
        key = rotated(packed_ref[:, columns(HEADS + head)])
        value = packed_ref[:, columns(2 * HEADS + head)]
        scores = jnp.where(same, dot_nt(query, key), -jnp.inf)
        top = jnp.max(scores, axis=-1, keepdims=True)
        expo = jnp.exp2((scores - top) * EXP2_SCALE).astype(BF16)
        both = dot_f32(expo, with_ones(value))
        result = both[:, :HEAD_DIM] / both[:, HEAD_DIM:]
        o_ref[:, first + head * HEAD_DIM : first + (head + 1) * HEAD_DIM] = result.astype(BF16)
    for copy in copies:
        copy.wait()


def temporal(packed, cosine, sine, group, following):
    rows = packed.shape[0]
    inner = HEADS * HEAD_DIM
    count = len(following)
    return pl.pallas_call(
        functools.partial(temporal_kernel, group),
        in_specs=[VMEM] * 3 + [HBM] * count,
        out_specs=VMEM,
        out_shape=jax.ShapeDtypeStruct((rows, inner * (1 + count)), BF16),
        scratch_shapes=[pltpu.SemaphoreType.DMA((3,))] if count else [],
        compiler_params=pltpu.CompilerParams(vmem_limit_bytes=6 * MIB),
        cost_estimate=pl.CostEstimate(
            flops=20_000_000_000 if count else 1, bytes_accessed=1, transcendentals=0
        ),
        name="temporal",
    )(packed, cosine, sine, *in_hbm(*following))


def project_rows(t_ref, hidden, w_out_ref, gain_ref, w_key_ref, w_value_ref, stream_ref, normed_ref, kv_ref, ready, done):
    inner, width = w_out_ref.shape
    part = 512
    squares = 0.0
    for i in range(width // part):
        at = slice(i * part, (i + 1) * part)
        ready(i)
        stream = (hidden[:, at].astype(F32) + dot_f32(t_ref[...], w_out_ref[:, at])).astype(BF16)
        stream_ref[:, at] = stream
        stream = stream.astype(F32)
        squares = squares + jnp.sum(stream * stream, axis=-1, keepdims=True)
    done(0)
    scale = lax.rsqrt(squares / width + 1e-06)
    normed_ref[...] = (stream_ref[...].astype(F32) * scale * gain_ref[...].astype(F32).reshape(1, width)).astype(BF16)
    done(1)
    for i in range(2 * inner // part):
        at = slice(i * part, (i + 1) * part)
        ready(width // part + i)
        w_ref = w_key_ref if i < inner // part else w_value_ref
        from_w = slice(i * part % inner, i * part % inner + part)
        kv_ref[:, at] = dot_f32(normed_ref[...], w_ref[:, from_w]).astype(BF16)
        done(2 + i)


def project_first_kernel(t_at, t_ref, hidden_ref, w_out_ref, gain_ref, w_key_ref, w_value_ref, *refs):
    outs, scratch, sems = refs[:3], refs[3:6], refs[6]
    rows = t_ref.shape[0]
    inner, width = w_out_ref.shape
    part = 512
    steps = 2 * inner // part
    cuts = [slice(i * part, (i + 1) * part) for i in range(steps)]
    copies = [pltpu.make_async_copy(scratch[i], outs[i], sems.at[i]) for i in range(2)]
    copies += [
        pltpu.make_async_copy(scratch[2].at[:, at], outs[2].at[:, at], sems.at[2 + i])
        for i, at in enumerate(cuts)
    ]

    project_rows(
        t_ref.at[:, t_at : t_at + inner],
        hidden_ref.at[:rows, :],
        w_out_ref,
        gain_ref,
        w_key_ref,
        w_value_ref,
        *scratch,
        lambda i: None,
        lambda i: copies[i].start(),
    )
    for copy in copies:
        copy.wait()


def project_first(t_out, t_at, hidden, w_out, gain, w_key, w_value):
    rows = t_out.shape[0]
    inner = HEADS * HEAD_DIM
    width = hidden.shape[1]
    shapes = [(rows, width), (rows, width), (rows, 2 * inner)]
    return pl.pallas_call(
        functools.partial(project_first_kernel, t_at),
        in_specs=[VMEM] * 6,
        out_specs=[HBM] * 3,
        out_shape=[pltpu.HBM(shape, BF16) for shape in shapes],
        scratch_shapes=[pltpu.VMEM(shape, BF16) for shape in shapes]
        + [pltpu.SemaphoreType.DMA((6,))],
        compiler_params=pltpu.CompilerParams(vmem_limit_bytes=10 * MIB),
        cost_estimate=pl.CostEstimate(flops=1, bytes_accessed=1, transcendentals=0),
        name="project_first",
    )(t_out, hidden, w_out, gain, w_key, w_value)


def project_second_kernel(t_ref, gain_ref, hidden_hbm, *refs):
    w_hbm, outs, hidden_ref, w_refs, sems = refs[:3], refs[3:6], refs[6], refs[7:10], refs[10]
    rows = t_ref.shape[0]
    part = 512
    get_hidden = pltpu.make_async_copy(hidden_hbm.at[rows:, :], hidden_ref, sems.at[8])
    get_hidden.start()
    copies = []
    for a, b in zip(w_hbm, w_refs):
        for i in range(a.shape[1] // part):
            at = slice(i * part, (i + 1) * part)
            copies.append(pltpu.make_async_copy(a.at[:, at], b.at[:, at], sems.at[len(copies)]))
            copies[-1].start()
    get_hidden.wait()
    project_rows(
        t_ref,
        hidden_ref,
        w_refs[0],
        gain_ref,
        w_refs[1],
        w_refs[2],
        *outs,
        lambda i: copies[i].wait(),
        lambda i: None,
    )


def project_second(t_out, hidden, w_out, gain, w_key, w_value):
    rows = t_out.shape[0]
    inner = HEADS * HEAD_DIM
    width = hidden.shape[1]
    shapes = [(rows, width), (rows, width), (rows, 2 * inner)]
    weights = (w_out, w_key, w_value)
    return pl.pallas_call(
        project_second_kernel,
        in_specs=[VMEM] * 2 + [HBM] * 4,
        out_specs=[VMEM] * 3,
        out_shape=[jax.ShapeDtypeStruct(shape, BF16) for shape in shapes],
        scratch_shapes=[pltpu.VMEM((rows, width), BF16)]
        + [pltpu.VMEM(w.shape, BF16) for w in weights]
        + [pltpu.SemaphoreType.DMA((9,))],
        compiler_params=pltpu.CompilerParams(vmem_limit_bytes=22 * MIB),
        cost_estimate=pl.CostEstimate(flops=1, bytes_accessed=1, transcendentals=0),
        name="project_second",
    )(t_out, gain, *in_hbm(hidden, *weights))


def first_kernel(sides, *refs):
    count = len(sides)
    normed_refs = refs[:2]
    w_query_ref, embed_ref = refs[2:4]
    kv_refs = refs[4 : 4 + count]
    q_ref, acc_ref, top_ref, total_ref = refs[4 + count :]
    inner = HEADS * HEAD_DIM
    rows = normed_refs[0].shape[0]
    for block, normed_ref in enumerate(normed_refs):
        q_ref[block * rows : (block + 1) * rows, :] = dot_f32(
            normed_ref[...], w_query_ref[...]
        ).astype(BF16)

    @pl.loop(0, HEADS)
    def _(head):
        at = pl.ds(pl.multiple_of(head * HEAD_DIM, HEAD_DIM), HEAD_DIM)
        value_at = pl.ds(pl.multiple_of(inner + head * HEAD_DIM, HEAD_DIM), HEAD_DIM)
        keys = []
        values = []
        for side, kv_ref in zip(sides, kv_refs):
            key = kv_ref[:, at]
            if side is not None:
                key = (key.astype(F32) + embed_ref[side : side + 1, at]).astype(BF16)
            keys.append(key)
            values.append(with_ones(kv_ref[:, value_at]))
        for block in range(2):
            here = slice(block * rows, (block + 1) * rows)
            query = q_ref[here, at]
            scores = [dot_nt(query, key) for key in keys]
            top = jnp.max(functools.reduce(jnp.maximum, scores), axis=-1, keepdims=True)
            acc = 0.0
            for score, value in zip(scores, values):
                acc = acc + dot_f32(jnp.exp2((score - top) * EXP2_SCALE).astype(BF16), value)
            acc_ref[here, at] = acc[:, :HEAD_DIM]
            total_ref[here, at] = acc[:, HEAD_DIM:]
            top_ref[here, at] = jnp.broadcast_to(top, (rows, HEAD_DIM))


def first_part(normed, w_query, embeds, views, sides):
    rows = 2 * normed[0].shape[0]
    inner, width = w_query.shape[1], w_query.shape[0]
    wide = jax.ShapeDtypeStruct((rows, inner), F32)
    return pl.pallas_call(
        functools.partial(first_kernel, sides),
        in_specs=[VMEM] * (4 + len(views)),
        out_specs=[VMEM] * 4,
        out_shape=[jax.ShapeDtypeStruct((rows, inner), BF16), wide, wide, wide],
        compiler_params=pltpu.CompilerParams(vmem_limit_bytes=12 * MIB),
        cost_estimate=pl.CostEstimate(
            flops=2 * rows * width * inner + 6 * rows * 256 * len(views) * inner,
            bytes_accessed=4 * MIB,
            transcendentals=rows * 256 * len(views) * HEADS,
        ),
        name="first_part",
    )(*normed, w_query, embeds, *views)


def last_kernel(
    q_ref, acc_ref, top_ref, total_ref, kv_ref, embed_ref, stream_a_ref, stream_b_ref, w_ref, o_ref, out_ref
):
    rows = stream_a_ref.shape[0]
    for block, stream_ref in enumerate((stream_a_ref, stream_b_ref)):
        here = slice(block * rows, (block + 1) * rows)
        for head in range(HEADS):
            at = columns(head)
            key = (kv_ref[:, at].astype(F32) + embed_ref[1:2, at]).astype(BF16)
            scores = dot_nt(q_ref[here, at], key)
            before = top_ref[here, at]
            top = jnp.maximum(before, jnp.max(scores, axis=-1, keepdims=True))
            keep = jnp.exp2((before - top) * EXP2_SCALE)
            expo = jnp.exp2((scores - jnp.concatenate([top, top], axis=1)) * EXP2_SCALE).astype(BF16)
            both = dot_f32(expo, with_ones(kv_ref[:, columns(HEADS + head)]))
            total = total_ref[here, at] * keep + both[:, HEAD_DIM:]
            acc = acc_ref[here, at] * keep + both[:, :HEAD_DIM]
            out_ref[here, at] = (acc / total).astype(BF16)
        product = dot_f32(out_ref[here, :], w_ref[...])
        o_ref[here, :] = (stream_ref[...].astype(F32) + product).astype(BF16)


def last_part(query, acc, top, total, view, embeds, streams, w_out):
    inner, width = w_out.shape
    rows = query.shape[0]
    return pl.pallas_call(
        last_kernel,
        in_specs=[VMEM] * 9,
        out_specs=VMEM,
        out_shape=jax.ShapeDtypeStruct((rows, width), BF16),
        scratch_shapes=[pltpu.VMEM((rows, inner), BF16)],
        compiler_params=pltpu.CompilerParams(vmem_limit_bytes=8 * MIB),
        cost_estimate=pl.CostEstimate(
            flops=2 * rows * width * inner + 6 * rows * view.shape[0] * inner,
            bytes_accessed=4 * MIB,
            transcendentals=rows * view.shape[0] * HEADS,
        ),
        name="last_part",
    )(query, acc, top, total, view, embeds, *streams, w_out)


def shards(
    hidden,
    t_query,
    t_key,
    t_value,
    frame_offsets,
    cycle_sides,
    w_temporal_out,
    norm_gain,
    w_query,
    w_key,
    w_value,
    w_cross_out,
    side_embed,
):
    rows_here = hidden.shape[2]
    model_width = hidden.shape[3]
    inner = t_query.shape[3]
    frames = lax.axis_size("frame")
    half = rows_here // 2
    group = half // frames
    hidden = hidden.reshape(rows_here, model_width)
    t_query = t_query.reshape(rows_here, inner)
    t_key = t_key.reshape(rows_here, inner)
    t_value = t_value.reshape(rows_here, inner)
    gain = norm_gain
    offsets = jnp.broadcast_to(frame_offsets.astype(F32)[:, None], (frames, HEAD_DIM))

    def exchange(value):
        return lax.all_to_all(value, "frame", split_axis=0, concat_axis=0, tiled=True)

    def to_near(value):
        return lax.ppermute(value, "cam", [(0, 1), (1, 0), (2, 3), (3, 2)])

    def to_far(value):
        return lax.ppermute(value, "cam", [(0, 3), (3, 0), (1, 2), (2, 1)])

    packed_a, cosine, sine = pack(t_query, t_key, t_value, offsets, rotary_frequencies())
    got_a = exchange(packed_a)
    weights = (w_temporal_out, gain, w_key, w_value)
    got_b = exchange(temporal(got_a, cosine, sine, group, [t_query, t_key, t_value]))
    stream_a, normed_a, kv_a = project_first(got_b, 3 * inner, hidden, *weights)
    far_a = to_far(kv_a)
    near_a = to_near(kv_a)
    got_b, kv_a = lax.optimization_barrier((got_b, kv_a))
    back_b = exchange(temporal(got_b, cosine, sine, group, []))
    stream_b, normed_b, kv_b = project_second(back_b, hidden, *weights)
    far_b = to_far(kv_b)
    near_b = to_near(kv_b)
    stream_b, cycle_sides, side_embed = lax.optimization_barrier((stream_b, cycle_sides, side_embed))
    near_cam = lax.axis_index("cam") ^ 1
    near_left = cycle_sides[0, 0] == near_cam
    side_f = side_embed.astype(F32)
    embeds = jnp.where(near_left, side_f, side_f[::-1])
    query, acc, top, total = first_part(
        [normed_a, normed_b], w_query, embeds, [kv_a, kv_b, near_a, near_b, far_a], (None, None, 0, 0, 1)
    )
    mixed = last_part(query, acc, top, total, far_b, embeds, [stream_a, stream_b], w_cross_out)
    return mixed.reshape(1, 1, rows_here, model_width)


def solution(mesh):
    in_specs = (
        P("cam", "frame", None, None),
        P("cam", "frame", None, None),
        P("cam", "frame", None, None),
        P("cam", "frame", None, None),
        P(),
        P("cam", None),
        P(),
        P(),
        P(),
        P(),
        P(),
        P(),
        P(),
    )
    out_specs = P("cam", "frame", None, None)
    return jax.shard_map(shards, mesh=mesh, in_specs=in_specs, out_specs=out_specs, check_vma=False)
```

```python
import functools
import math

import jax
import jax.numpy as jnp
from jax import lax
from jax.experimental import pallas as pl
from jax.experimental.pallas import tpu as pltpu
from jax.sharding import PartitionSpec as P

HEADS = 8
HEAD_DIM = 128
MIB = 1 << 20
F32 = jnp.float32
BF16 = jnp.bfloat16
EXP2_SCALE = math.log2(math.e) / math.sqrt(HEAD_DIM)


def dot_f32(a, b):
    return jnp.dot(a, b, preferred_element_type=F32)


def dot_nt(a, b):
    return lax.dot_general(a, b, (((1,), (1,)), ((), ())), preferred_element_type=F32)


def rotary_frequencies():
    half_dim = HEAD_DIM // 2
    steps_f = jnp.arange(half_dim).astype(F32)
    frequencies = 10000.0 ** (-steps_f / half_dim)
    return jnp.concatenate([frequencies, frequencies])[None, :]


VMEM = pl.BlockSpec(memory_space=pltpu.VMEM)
HBM = pl.BlockSpec(memory_space=pltpu.HBM)


def columns(head):
    return slice(head * HEAD_DIM, (head + 1) * HEAD_DIM)


def with_ones(values):
    return jnp.concatenate([values, jnp.ones_like(values)], axis=1)


def copy_all(pairs, sems):
    copies = [pltpu.make_async_copy(a, b, sems.at[i]) for i, (a, b) in enumerate(pairs)]
    for copy in copies:
        copy.start()
    for copy in copies:
        copy.wait()


def in_hbm(*arrays):
    return [pltpu.with_memory_space_constraint(array, pltpu.HBM) for array in arrays]


def pack_kernel(q_ref, k_ref, v_ref, offset_ref, frequency_ref, o_ref, cos_ref, sin_ref, sems):
    rows, inner = o_ref.shape[0], q_ref.shape[1]
    moves = [
        pltpu.make_async_copy(ref.at[:rows, :], o_ref.at[:, i * inner : (i + 1) * inner], sems.at[i])
        for i, ref in enumerate((q_ref, k_ref, v_ref))
    ]
    for move in moves:
        move.start()
    frames = offset_ref.shape[0]
    group = rows // frames
    angles = offset_ref[...] * frequency_ref[...]
    lane = lax.broadcasted_iota(jnp.int32, angles.shape, 1)
    cosine = jnp.cos(angles)
    sine = jnp.sin(angles)
    sine = jnp.where(lane < HEAD_DIM // 2, -sine, sine)
    for frame in range(frames):
        at = slice(frame * group, (frame + 1) * group)
        cos_ref[at, :] = jnp.broadcast_to(cosine[frame : frame + 1, :], (group, HEAD_DIM))
        sin_ref[at, :] = jnp.broadcast_to(sine[frame : frame + 1, :], (group, HEAD_DIM))
    for move in moves:
        move.wait()


def pack(query, key, value, offsets, frequencies):
    rows, inner = query.shape
    half = rows // 2
    table = pltpu.VMEM((half, HEAD_DIM), F32)
    return pl.pallas_call(
        pack_kernel,
        in_specs=[HBM] * 3 + [VMEM] * 2,
        out_specs=[VMEM] * 3,
        out_shape=[pltpu.VMEM((half, 3 * inner), BF16), table, table],
        scratch_shapes=[pltpu.SemaphoreType.DMA((3,))],
        compiler_params=pltpu.CompilerParams(vmem_limit_bytes=4 * MIB),
        cost_estimate=pl.CostEstimate(flops=0, bytes_accessed=6 * rows * inner, transcendentals=0),
        name="pack",
    )(*in_hbm(query, key, value), offsets, frequencies)


def temporal_kernel(group, packed_ref, cos_ref, sin_ref, *refs):
    rows = packed_ref.shape[0]
    inner = HEADS * HEAD_DIM
    count = len(refs) - 3 if len(refs) > 3 else 0
    first = 0
    copies = []
    if not count:
        o_hbm, o_ref, sems = refs
    else:
        o_ref = refs[count]
        first = count * inner
        for i, ref in enumerate(refs[:count]):
            to = o_ref.at[:, i * inner : (i + 1) * inner]
            copies.append(pltpu.make_async_copy(ref.at[rows:, :], to, refs[count + 2].at[i]))
            copies[-1].start()
    cosine = cos_ref[...]
    sine = sin_ref[...]
    row_at = lax.broadcasted_iota(jnp.int32, (rows, rows), 0)
    key_at = lax.broadcasted_iota(jnp.int32, (rows, rows), 1)
    same = lax.rem(row_at, group) == lax.rem(key_at, group)
    def rotated(part):
        part = part.astype(F32)
        return (part * cosine + pltpu.roll(part, HEAD_DIM // 2, 1) * sine).astype(BF16)

    for head in range(HEADS):
        query = rotated(packed_ref[:, columns(head)])
        key = rotated(packed_ref[:, columns(HEADS + head)])
        value = packed_ref[:, columns(2 * HEADS + head)]
        scores = jnp.where(same, dot_nt(query, key), -jnp.inf)
        top = jnp.max(scores, axis=-1, keepdims=True)
        expo = jnp.exp2((scores - top) * EXP2_SCALE).astype(BF16)
        both = dot_f32(expo, with_ones(value))
        result = both[:, :HEAD_DIM] / both[:, HEAD_DIM:]
        o_ref[:, first + head * HEAD_DIM : first + (head + 1) * HEAD_DIM] = result.astype(BF16)
        if not count and head % 4 == 3:
            at = slice((head - 3) * HEAD_DIM, (head + 1) * HEAD_DIM)
            copies.append(pltpu.make_async_copy(o_ref.at[:, at], o_hbm.at[:, at], sems.at[head // 4]))
            copies[-1].start()
    for copy in copies:
        copy.wait()


def temporal(packed, cosine, sine, group, following):
    rows = packed.shape[0]
    inner = HEADS * HEAD_DIM
    count = len(following)
    shape = (rows, inner * (1 + count))
    return pl.pallas_call(
        functools.partial(temporal_kernel, group),
        in_specs=[VMEM] * 3 + [HBM] * count,
        out_specs=VMEM if count else HBM,
        out_shape=jax.ShapeDtypeStruct(shape, BF16) if count else pltpu.HBM(shape, BF16),
        scratch_shapes=[pltpu.VMEM((8, 128) if count else shape, BF16), pltpu.SemaphoreType.DMA((3,))],
        compiler_params=pltpu.CompilerParams(vmem_limit_bytes=6 * MIB),
        cost_estimate=pl.CostEstimate(
            flops=20_000_000_000 if count else 1, bytes_accessed=1, transcendentals=0
        ),
        name="temporal",
    )(packed, cosine, sine, *in_hbm(*following))


def project_rows(t_ref, hidden, w_out_ref, gain_ref, w_key_ref, w_value_ref, stream_ref, normed_ref, kv_ref, ready, done):
    inner, width = w_out_ref.shape
    part = 512
    squares = 0.0
    for i in range(width // part):
        at = slice(i * part, (i + 1) * part)
        ready(i)
        stream = (hidden[:, at].astype(F32) + dot_f32(t_ref[...], w_out_ref[:, at])).astype(BF16)
        stream_ref[:, at] = stream
        stream = stream.astype(F32)
        squares = squares + jnp.sum(stream * stream, axis=-1, keepdims=True)
    done(0)
    scale = lax.rsqrt(squares / width + 1e-06)
    normed_ref[...] = (stream_ref[...].astype(F32) * scale * gain_ref[...].astype(F32).reshape(1, width)).astype(BF16)
    done(1)
    for i in range(2 * inner // part):
        at = slice(i * part, (i + 1) * part)
        ready(width // part + i)
        w_ref = w_key_ref if i < inner // part else w_value_ref
        from_w = slice(i * part % inner, i * part % inner + part)
        kv_ref[:, at] = dot_f32(normed_ref[...], w_ref[:, from_w]).astype(BF16)
        done(2 + i)


def project_first_kernel(t_at, t_ref, hidden_ref, w_out_ref, gain_ref, w_key_ref, w_value_ref, *refs):
    outs, alone, scratch, sems = refs[:3], refs[3:5], refs[5:8], refs[8]
    rows = t_ref.shape[0]
    inner, width = w_out_ref.shape
    part = 512
    steps = 2 * inner // part
    cuts = [slice(i * part, (i + 1) * part) for i in range(steps)]
    copies = [pltpu.make_async_copy(scratch[i], outs[i], sems.at[i]) for i in range(2)]
    copies += [
        pltpu.make_async_copy(scratch[2].at[:, at], outs[2].at[:, at], sems.at[2 + i])
        for i, at in enumerate(cuts)
    ]


    def done(i):
        copies[i].start()
        if i >= 2:
            j = i - 2
            to = alone[j // (steps // 2)].at[:, cuts[j % (steps // 2)]]
            copies.append(pltpu.make_async_copy(scratch[2].at[:, cuts[j]], to, sems.at[2 + steps + j]))
            copies[-1].start()

    project_rows(
        t_ref.at[:, t_at : t_at + inner],
        hidden_ref.at[:rows, :],
        w_out_ref,
        gain_ref,
        w_key_ref,
        w_value_ref,
        *scratch,
        lambda i: None,
        done,
    )
    for copy in copies:
        copy.wait()


def project_first(t_out, t_at, hidden, w_out, gain, w_key, w_value):
    rows = t_out.shape[0]
    inner = HEADS * HEAD_DIM
    width = hidden.shape[1]
    shapes = [(rows, width), (rows, width), (rows, 2 * inner)]
    return pl.pallas_call(
        functools.partial(project_first_kernel, t_at),
        in_specs=[VMEM] * 6,
        out_specs=[HBM] * 5,
        out_shape=[pltpu.HBM(shape, BF16) for shape in shapes + [(rows, inner)] * 2],
        scratch_shapes=[pltpu.VMEM(shape, BF16) for shape in shapes]
        + [pltpu.SemaphoreType.DMA((10,))],
        compiler_params=pltpu.CompilerParams(vmem_limit_bytes=10 * MIB),
        cost_estimate=pl.CostEstimate(flops=1, bytes_accessed=1, transcendentals=0),
        name="project_first",
    )(t_out, hidden, w_out, gain, w_key, w_value)


def project_second_kernel(t_ref, gain_ref, hidden_hbm, *refs):
    w_hbm, outs, hidden_ref, normed_ref, kv_ref = refs[:3], refs[3:6], refs[6], refs[7], refs[8]
    w_refs, sems = refs[9:12], refs[12]
    rows = t_ref.shape[0]
    part = 512
    get_hidden = pltpu.make_async_copy(hidden_hbm.at[rows:, :], hidden_ref, sems.at[8])
    get_hidden.start()
    copies = []
    for a, b in zip(w_hbm, w_refs):
        for i in range(a.shape[1] // part):
            at = slice(i * part, (i + 1) * part)
            copies.append(pltpu.make_async_copy(a.at[:, at], b.at[:, at], sems.at[len(copies)]))
            copies[-1].start()
    leaving = []

    def done(i):
        if i == 1:
            leaving.append(pltpu.make_async_copy(normed_ref, outs[1], sems.at[13]))
            leaving[-1].start()
        if i >= 2:
            at = slice((i - 2) * part, (i - 1) * part)
            copy = pltpu.make_async_copy(kv_ref.at[:, at], outs[2].at[:, at], sems.at[7 + i])
            leaving.append(copy)
            copy.start()

    get_hidden.wait()
    project_rows(
        t_ref,
        hidden_ref,
        w_refs[0],
        gain_ref,
        w_refs[1],
        w_refs[2],
        outs[0],
        normed_ref,
        kv_ref,
        lambda i: copies[i].wait(),
        done,
    )
    for copy in leaving:
        copy.wait()


def project_second(t_out, hidden, w_out, gain, w_key, w_value):
    rows = t_out.shape[0]
    inner = HEADS * HEAD_DIM
    width = hidden.shape[1]
    shapes = [(rows, width), (rows, width), (rows, 2 * inner)]
    weights = (w_out, w_key, w_value)
    return pl.pallas_call(
        project_second_kernel,
        in_specs=[VMEM] * 2 + [HBM] * 4,
        out_specs=[VMEM] + [HBM] * 2,
        out_shape=[jax.ShapeDtypeStruct(shapes[0], BF16)]
        + [pltpu.HBM(shape, BF16) for shape in shapes[1:]],
        scratch_shapes=[pltpu.VMEM((rows, width), BF16)]
        + [pltpu.VMEM(shape, BF16) for shape in shapes[1:]]
        + [pltpu.VMEM(w.shape, BF16) for w in weights]
        + [pltpu.SemaphoreType.DMA((14,))],
        compiler_params=pltpu.CompilerParams(vmem_limit_bytes=24 * MIB),
        cost_estimate=pl.CostEstimate(flops=1, bytes_accessed=1, transcendentals=0),
        name="project_second",
    )(t_out, gain, *in_hbm(hidden, *weights))


def first_kernel(embed_ref, *refs):
    from_hbm, (q_ref, acc_ref, top_ref, total_ref), held, sems = refs[:9], refs[9:13], refs[13:22], refs[22]
    normed_refs, w_ref, own_and_near, (far_k_ref, far_v_ref) = held[:2], held[2], held[3:7], held[7:9]
    rows = normed_refs[0].shape[0]
    part = 256
    parts = w_ref.shape[1] // part

    def fetch(i):
        copy = pltpu.make_async_copy(from_hbm[i], held[i], sems.at[i])
        copy.start()
        return copy

    w_copies = []
    arrivals = [fetch(0)]
    for i in range(parts):
        at = slice(i * part, (i + 1) * part)
        w_copies.append(
            pltpu.make_async_copy(from_hbm[2].at[:, at], w_ref.at[:, at], sems.at[9 + i])
        )
        w_copies[-1].start()
    arrivals += [fetch(1)] + [fetch(i) for i in range(3, 9)]
    arrivals[0].wait()
    for i in range(parts):
        at = slice(i * part, (i + 1) * part)
        w_copies[i].wait()
        q_ref[:rows, at] = dot_f32(normed_refs[0][...], w_ref[:, at]).astype(BF16)
    arrivals[1].wait()
    q_ref[rows:, :] = dot_f32(normed_refs[1][...], w_ref[...]).astype(BF16)
    for copy in arrivals[2:]:
        copy.wait()
    for head in range(HEADS):
        at = columns(head)
        keys = [kv_ref[:, at] for kv_ref in own_and_near] + [far_k_ref[:, at]]
        values = [kv_ref[:, columns(HEADS + head)] for kv_ref in own_and_near] + [far_v_ref[:, at]]
        values = [with_ones(value) for value in values]
        for i, side in ((2, 0), (3, 0), (4, 1)):
            keys[i] = (keys[i].astype(F32) + embed_ref[side : side + 1, at]).astype(BF16)
        for block in range(2):
            here = slice(block * rows, (block + 1) * rows)
            query = q_ref[here, at]
            scores = [dot_nt(query, key) for key in keys]
            top = jnp.max(functools.reduce(jnp.maximum, scores), axis=-1, keepdims=True)
            acc = 0.0
            for score, value in zip(scores, values):
                acc = acc + dot_f32(jnp.exp2((score - top) * EXP2_SCALE).astype(BF16), value)
            acc_ref[here, at] = acc[:, :HEAD_DIM]
            total_ref[here, at] = acc[:, HEAD_DIM:]
            top_ref[here, at] = jnp.broadcast_to(top, (rows, HEAD_DIM))


def first_part(normed, w_query, embeds, own, near, far_key, far_value):
    rows = 2 * normed[0].shape[0]
    inner, width = w_query.shape[1], w_query.shape[0]
    wide = jax.ShapeDtypeStruct((rows, inner), F32)
    fetched = [*normed, w_query, *own, *near, far_key, far_value]
    return pl.pallas_call(
        first_kernel,
        in_specs=[VMEM] + [HBM] * len(fetched),
        out_specs=[VMEM] * 4,
        out_shape=[jax.ShapeDtypeStruct((rows, inner), BF16), wide, wide, wide],
        scratch_shapes=[pltpu.VMEM(array.shape, BF16) for array in fetched]
        + [pltpu.SemaphoreType.DMA((13,))],
        compiler_params=pltpu.CompilerParams(vmem_limit_bytes=24 * MIB),
        cost_estimate=pl.CostEstimate(
            flops=2 * rows * width * inner + 30 * rows * 256 * inner,
            bytes_accessed=4 * MIB,
            transcendentals=rows * 256 * 5 * HEADS,
        ),
        name="first_part",
    )(embeds, *in_hbm(*fetched))


def last_kernel(
    q_ref, acc_ref, top_ref, total_ref, kv_ref, embed_ref, stream_a_ref, stream_b_ref, w_ref, o_ref, out_ref
):
    rows = stream_a_ref.shape[0]
    for block, stream_ref in enumerate((stream_a_ref, stream_b_ref)):
        here = slice(block * rows, (block + 1) * rows)
        for head in range(HEADS):
            at = columns(head)
            key = (kv_ref[:, at].astype(F32) + embed_ref[1:2, at]).astype(BF16)
            scores = dot_nt(q_ref[here, at], key)
            before = top_ref[here, at]
            top = jnp.maximum(before, jnp.max(scores, axis=-1, keepdims=True))
            keep = jnp.exp2((before - top) * EXP2_SCALE)
            expo = jnp.exp2((scores - jnp.concatenate([top, top], axis=1)) * EXP2_SCALE).astype(BF16)
            both = dot_f32(expo, with_ones(kv_ref[:, columns(HEADS + head)]))
            total = total_ref[here, at] * keep + both[:, HEAD_DIM:]
            acc = acc_ref[here, at] * keep + both[:, :HEAD_DIM]
            out_ref[here, at] = (acc / total).astype(BF16)
        product = dot_f32(out_ref[here, :], w_ref[...])
        o_ref[here, :] = (stream_ref[...].astype(F32) + product).astype(BF16)


def last_part(query, acc, top, total, view, embeds, streams, w_out):
    inner, width = w_out.shape
    rows = query.shape[0]
    return pl.pallas_call(
        last_kernel,
        in_specs=[VMEM] * 9,
        out_specs=VMEM,
        out_shape=jax.ShapeDtypeStruct((rows, width), BF16),
        scratch_shapes=[pltpu.VMEM((rows, inner), BF16)],
        compiler_params=pltpu.CompilerParams(vmem_limit_bytes=8 * MIB),
        cost_estimate=pl.CostEstimate(
            flops=2 * rows * width * inner + 6 * rows * view.shape[0] * inner,
            bytes_accessed=4 * MIB,
            transcendentals=rows * view.shape[0] * HEADS,
        ),
        name="last_part",
    )(query, acc, top, total, view, embeds, *streams, w_out)


def shards(
    hidden,
    t_query,
    t_key,
    t_value,
    frame_offsets,
    cycle_sides,
    w_temporal_out,
    norm_gain,
    w_query,
    w_key,
    w_value,
    w_cross_out,
    side_embed,
):
    rows_here = hidden.shape[2]
    model_width = hidden.shape[3]
    inner = t_query.shape[3]
    frames = lax.axis_size("frame")
    half = rows_here // 2
    group = half // frames
    hidden = hidden.reshape(rows_here, model_width)
    t_query = t_query.reshape(rows_here, inner)
    t_key = t_key.reshape(rows_here, inner)
    t_value = t_value.reshape(rows_here, inner)
    gain = norm_gain
    offsets = jnp.broadcast_to(frame_offsets.astype(F32)[:, None], (frames, HEAD_DIM))

    def exchange(value):
        return lax.all_to_all(value, "frame", split_axis=0, concat_axis=0, tiled=True)

    def to_near(value):
        return lax.ppermute(value, "cam", [(0, 1), (1, 0), (2, 3), (3, 2)])

    def to_far(value):
        return lax.ppermute(value, "cam", [(0, 3), (3, 0), (1, 2), (2, 1)])

    packed_a, cosine, sine = pack(t_query, t_key, t_value, offsets, rotary_frequencies())
    got_a = exchange(packed_a)
    weights = (w_temporal_out, gain, w_key, w_value)
    got_b = exchange(temporal(got_a, cosine, sine, group, [t_query, t_key, t_value]))
    stream_a, normed_a, kv_a, key_a, value_a = project_first(got_b, 3 * inner, hidden, *weights)
    far_key_a = to_far(key_a)
    far_key_a, value_a = lax.optimization_barrier((far_key_a, value_a))
    far_value_a = to_far(value_a)
    near_a = to_near(kv_a)
    got_b, key_a = lax.optimization_barrier((got_b, key_a))
    back_b = exchange(temporal(got_b, cosine, sine, group, []))
    stream_b, normed_b, kv_b = project_second(back_b, hidden, *weights)
    far_b = to_far(kv_b)
    near_b = to_near(kv_b)
    token = side_embed[:, :HEAD_DIM]
    far_value_a, token = lax.optimization_barrier((far_value_a, token))
    token = to_near(token)
    token = to_near(token + 1)
    stream_b, cycle_sides, side_embed = lax.optimization_barrier((stream_b, cycle_sides, side_embed))
    near_cam = lax.axis_index("cam") ^ 1
    near_left = cycle_sides[0, 0] == near_cam
    side_f = side_embed.astype(F32)
    embeds = jnp.where(near_left, side_f, side_f[::-1])
    embeds, token = lax.optimization_barrier((embeds, token))
    embeds = embeds + 0.0 * token[:1, :1].astype(F32)
    query, acc, top, total = first_part(
        [normed_a, normed_b], w_query, embeds, [kv_a, kv_b], [near_a, near_b], far_key_a, far_value_a
    )
    mixed = last_part(query, acc, top, total, far_b, embeds, [stream_a, stream_b], w_cross_out)
    return mixed.reshape(1, 1, rows_here, model_width)


def solution(mesh):
    in_specs = (
        P("cam", "frame", None, None),
        P("cam", "frame", None, None),
        P("cam", "frame", None, None),
        P("cam", "frame", None, None),
        P(),
        P("cam", None),
        P(),
        P(),
        P(),
        P(),
        P(),
        P(),
        P(),
    )
    out_specs = P("cam", "frame", None, None)
    return jax.shard_map(shards, mesh=mesh, in_specs=in_specs, out_specs=out_specs, check_vma=False)
```

```python
import functools
import math

import jax
import jax.numpy as jnp
from jax import lax
from jax.experimental import pallas as pl
from jax.experimental.pallas import tpu as pltpu
from jax.sharding import PartitionSpec as P

HEADS = 8
HEAD_DIM = 128
MIB = 1 << 20
F32 = jnp.float32
BF16 = jnp.bfloat16
EXP2_SCALE = math.log2(math.e) / math.sqrt(HEAD_DIM)


def dot_f32(a, b):
    return jnp.dot(a, b, preferred_element_type=F32)


def dot_nt(a, b):
    return lax.dot_general(a, b, (((1,), (1,)), ((), ())), preferred_element_type=F32)


FIRST_PIECE = 1536
KV_CUTS = [slice(0, 512), slice(512, 1024), slice(1024, 1536), slice(1536, 2048)]


def alone_part(refs, at, split):
    second = at.start >= split
    first = at.start - split * second
    return refs[second].at[:, first : first + at.stop - at.start]


def rotary_frequencies():
    half_dim = HEAD_DIM // 2
    steps_f = jnp.arange(half_dim).astype(F32)
    frequencies = 10000.0 ** (-steps_f / half_dim)
    return jnp.concatenate([frequencies, frequencies])[None, :]


VMEM = pl.BlockSpec(memory_space=pltpu.VMEM)
HBM = pl.BlockSpec(memory_space=pltpu.HBM)


def columns(head):
    return slice(head * HEAD_DIM, (head + 1) * HEAD_DIM)


def with_ones(values):
    return jnp.concatenate([values, jnp.ones_like(values)], axis=1)


def copy_all(pairs, sems):
    copies = [pltpu.make_async_copy(a, b, sems.at[i]) for i, (a, b) in enumerate(pairs)]
    for copy in copies:
        copy.start()
    for copy in copies:
        copy.wait()


def in_hbm(*arrays):
    return [pltpu.with_memory_space_constraint(array, pltpu.HBM) for array in arrays]


def pack_kernel(q_ref, k_ref, v_ref, offset_ref, frequency_ref, o_ref, cos_ref, sin_ref, sems):
    rows, inner = o_ref.shape[0], q_ref.shape[1]
    moves = [
        pltpu.make_async_copy(ref.at[:rows, :], o_ref.at[:, i * inner : (i + 1) * inner], sems.at[i])
        for i, ref in enumerate((q_ref, k_ref, v_ref))
    ]
    for move in moves:
        move.start()
    frames = offset_ref.shape[0]
    group = rows // frames
    angles = offset_ref[...] * frequency_ref[...]
    lane = lax.broadcasted_iota(jnp.int32, angles.shape, 1)
    cosine = jnp.cos(angles)
    sine = jnp.sin(angles)
    sine = jnp.where(lane < HEAD_DIM // 2, -sine, sine)
    for frame in range(frames):
        at = slice(frame * group, (frame + 1) * group)
        cos_ref[at, :] = jnp.broadcast_to(cosine[frame : frame + 1, :], (group, HEAD_DIM))
        sin_ref[at, :] = jnp.broadcast_to(sine[frame : frame + 1, :], (group, HEAD_DIM))
    for move in moves:
        move.wait()


def pack(query, key, value, offsets, frequencies):
    rows, inner = query.shape
    half = rows // 2
    table = pltpu.VMEM((half, HEAD_DIM), F32)
    return pl.pallas_call(
        pack_kernel,
        in_specs=[HBM] * 3 + [VMEM] * 2,
        out_specs=[VMEM] * 3,
        out_shape=[pltpu.VMEM((half, 3 * inner), BF16), table, table],
        scratch_shapes=[pltpu.SemaphoreType.DMA((3,))],
        compiler_params=pltpu.CompilerParams(vmem_limit_bytes=4 * MIB),
        cost_estimate=pl.CostEstimate(flops=0, bytes_accessed=6 * rows * inner, transcendentals=0),
        name="pack",
    )(*in_hbm(query, key, value), offsets, frequencies)


def temporal_kernel(group, packed_ref, cos_ref, sin_ref, *refs):
    rows = packed_ref.shape[0]
    inner = HEADS * HEAD_DIM
    count = len(refs) - 3 if len(refs) > 3 else 0
    first = 0
    copies = []
    if not count:
        o_hbm, o_ref, sems = refs
    else:
        o_ref = refs[count]
        first = count * inner
        for i, ref in enumerate(refs[:count]):
            to = o_ref.at[:, i * inner : (i + 1) * inner]
            copies.append(pltpu.make_async_copy(ref.at[rows:, :], to, refs[count + 2].at[i]))
            copies[-1].start()
    cosine = cos_ref[...]
    sine = sin_ref[...]
    row_at = lax.broadcasted_iota(jnp.int32, (rows, rows), 0)
    key_at = lax.broadcasted_iota(jnp.int32, (rows, rows), 1)
    same = lax.rem(row_at, group) == lax.rem(key_at, group)
    def rotated(part):
        part = part.astype(F32)
        return (part * cosine + pltpu.roll(part, HEAD_DIM // 2, 1) * sine).astype(BF16)

    for head in range(HEADS):
        query = rotated(packed_ref[:, columns(head)])
        key = rotated(packed_ref[:, columns(HEADS + head)])
        value = packed_ref[:, columns(2 * HEADS + head)]
        scores = jnp.where(same, dot_nt(query, key), -jnp.inf)
        top = jnp.max(scores, axis=-1, keepdims=True)
        expo = jnp.exp2((scores - top) * EXP2_SCALE).astype(BF16)
        both = dot_f32(expo, with_ones(value))
        result = both[:, :HEAD_DIM] / both[:, HEAD_DIM:]
        o_ref[:, first + head * HEAD_DIM : first + (head + 1) * HEAD_DIM] = result.astype(BF16)
        if not count and head % 4 == 3:
            at = slice((head - 3) * HEAD_DIM, (head + 1) * HEAD_DIM)
            copies.append(pltpu.make_async_copy(o_ref.at[:, at], o_hbm.at[:, at], sems.at[head // 4]))
            copies[-1].start()
    for copy in copies:
        copy.wait()


def temporal(packed, cosine, sine, group, following):
    rows = packed.shape[0]
    inner = HEADS * HEAD_DIM
    count = len(following)
    shape = (rows, inner * (1 + count))
    return pl.pallas_call(
        functools.partial(temporal_kernel, group),
        in_specs=[VMEM] * 3 + [HBM] * count,
        out_specs=VMEM if count else HBM,
        out_shape=jax.ShapeDtypeStruct(shape, BF16) if count else pltpu.HBM(shape, BF16),
        scratch_shapes=[pltpu.VMEM((8, 128) if count else shape, BF16), pltpu.SemaphoreType.DMA((3,))],
        compiler_params=pltpu.CompilerParams(vmem_limit_bytes=6 * MIB),
        cost_estimate=pl.CostEstimate(
            flops=20_000_000_000 if count else 1, bytes_accessed=1, transcendentals=0
        ),
        name="temporal",
    )(packed, cosine, sine, *in_hbm(*following))


def project_rows(t_ref, hidden, w_out_ref, gain_ref, w_key_ref, w_value_ref, stream_ref, normed_ref, kv_ref, ready, done):
    inner, width = w_out_ref.shape
    part = 512
    squares = 0.0
    for i in range(width // part):
        at = slice(i * part, (i + 1) * part)
        ready(i)
        stream = (hidden[:, at].astype(F32) + dot_f32(t_ref[...], w_out_ref[:, at])).astype(BF16)
        stream_ref[:, at] = stream
        stream = stream.astype(F32)
        squares = squares + jnp.sum(stream * stream, axis=-1, keepdims=True)
    done(0)
    scale = lax.rsqrt(squares / width + 1e-06)
    normed_ref[...] = (stream_ref[...].astype(F32) * scale * gain_ref[...].astype(F32).reshape(1, width)).astype(BF16)
    done(1)
    for i, at in enumerate(KV_CUTS):
        ready(width // part + i)
        w_ref = w_key_ref if at.start < inner else w_value_ref
        from_w = slice(at.start % inner, at.start % inner + at.stop - at.start)
        kv_ref[:, at] = dot_f32(normed_ref[...], w_ref[:, from_w]).astype(BF16)
        done(2 + i)


def project_first_kernel(t_at, t_ref, hidden_ref, w_out_ref, gain_ref, w_key_ref, w_value_ref, *refs):
    outs, alone, scratch, sems = refs[:3], refs[3:5], refs[5:8], refs[8]
    rows = t_ref.shape[0]
    inner = w_out_ref.shape[0]
    copies = []

    def leave(a, b):
        copies.append(pltpu.make_async_copy(a, b, sems.at[len(copies)]))
        copies[-1].start()

    def done(i):
        if i < 2:
            leave(scratch[i], outs[i])
        else:
            at = KV_CUTS[i - 2]
            leave(scratch[2].at[:, at], alone_part(alone, at, inner))
            leave(scratch[2].at[:, at], outs[2].at[:, at])

    project_rows(
        t_ref.at[:, t_at : t_at + inner],
        hidden_ref.at[:rows, :],
        w_out_ref,
        gain_ref,
        w_key_ref,
        w_value_ref,
        *scratch,
        lambda i: None,
        done,
    )
    for copy in copies:
        copy.wait()


def project_first(t_out, t_at, hidden, w_out, gain, w_key, w_value):
    rows = t_out.shape[0]
    inner = HEADS * HEAD_DIM
    width = hidden.shape[1]
    shapes = [(rows, width), (rows, width), (rows, 2 * inner)]
    return pl.pallas_call(
        functools.partial(project_first_kernel, t_at),
        in_specs=[VMEM] * 6,
        out_specs=[HBM] * 5,
        out_shape=[pltpu.HBM(shape, BF16) for shape in shapes + [(rows, inner)] * 2],
        scratch_shapes=[pltpu.VMEM(shape, BF16) for shape in shapes]
        + [pltpu.SemaphoreType.DMA((12,))],
        compiler_params=pltpu.CompilerParams(vmem_limit_bytes=10 * MIB),
        cost_estimate=pl.CostEstimate(flops=1, bytes_accessed=1, transcendentals=0),
        name="project_first",
    )(t_out, hidden, w_out, gain, w_key, w_value)


def project_second_kernel(t_ref, gain_ref, hidden_hbm, *refs):
    w_hbm, outs, alone, hidden_ref, normed_ref, kv_ref = refs[:3], refs[3:6], refs[6:8], *refs[8:11]
    w_refs, arrived, left = refs[11:14], refs[14], refs[15]
    rows = t_ref.shape[0]
    inner = HEADS * HEAD_DIM
    part = 512
    get_hidden = pltpu.make_async_copy(hidden_hbm.at[rows:, :], hidden_ref, arrived.at[9])
    get_hidden.start()
    cuts = [(0, slice(i, i + part)) for i in range(0, w_hbm[0].shape[1], part)]
    for at in KV_CUTS:
        first = at.start % inner
        cuts.append((1 + at.start // inner, slice(first, first + at.stop - at.start)))
    copies = []
    for i, (which, at) in enumerate(cuts):
        copies.append(
            pltpu.make_async_copy(w_hbm[which].at[:, at], w_refs[which].at[:, at], arrived.at[i])
        )
        copies[-1].start()
    leaving = []

    def leave(a, b):
        leaving.append(pltpu.make_async_copy(a, b, left.at[len(leaving)]))
        leaving[-1].start()

    def done(i):
        if i == 1:
            leave(normed_ref, outs[1])
        if i >= 2:
            at = KV_CUTS[i - 2]
            leave(kv_ref.at[:, at], alone_part(alone, at, FIRST_PIECE))
            leave(kv_ref.at[:, at], outs[2].at[:, at])

    get_hidden.wait()
    project_rows(
        t_ref,
        hidden_ref,
        w_refs[0],
        gain_ref,
        w_refs[1],
        w_refs[2],
        outs[0],
        normed_ref,
        kv_ref,
        lambda i: copies[i].wait(),
        done,
    )
    for copy in leaving:
        copy.wait()


def project_second(t_out, hidden, w_out, gain, w_key, w_value):
    rows = t_out.shape[0]
    inner = HEADS * HEAD_DIM
    width = hidden.shape[1]
    shapes = [(rows, width), (rows, width), (rows, 2 * inner)]
    weights = (w_out, w_key, w_value)
    return pl.pallas_call(
        project_second_kernel,
        in_specs=[VMEM] * 2 + [HBM] * 4,
        out_specs=[VMEM] + [HBM] * 4,
        out_shape=[jax.ShapeDtypeStruct(shapes[0], BF16)]
        + [
            pltpu.HBM(shape, BF16)
            for shape in shapes[1:] + [(rows, FIRST_PIECE), (rows, 2 * inner - FIRST_PIECE)]
        ],
        scratch_shapes=[pltpu.VMEM((rows, width), BF16)]
        + [pltpu.VMEM(shape, BF16) for shape in shapes[1:]]
        + [pltpu.VMEM(w.shape, BF16) for w in weights]
        + [pltpu.SemaphoreType.DMA((10,)), pltpu.SemaphoreType.DMA((11,))],
        compiler_params=pltpu.CompilerParams(vmem_limit_bytes=24 * MIB),
        cost_estimate=pl.CostEstimate(flops=1, bytes_accessed=1, transcendentals=0),
        name="project_second",
    )(t_out, gain, *in_hbm(hidden, *weights))


def first_kernel(embed_ref, *refs):
    from_hbm, (q_ref, acc_ref, top_ref, total_ref), held, sems = refs[:9], refs[9:13], refs[13:22], refs[22]
    normed_refs, w_ref, own_and_near, (far_k_ref, far_v_ref) = held[:2], held[2], held[3:7], held[7:9]
    rows = normed_refs[0].shape[0]
    part = 256
    parts = w_ref.shape[1] // part

    def fetch(i):
        copy = pltpu.make_async_copy(from_hbm[i], held[i], sems.at[i])
        copy.start()
        return copy

    w_copies = []
    arrivals = [fetch(0)]
    for i in range(parts):
        at = slice(i * part, (i + 1) * part)
        w_copies.append(
            pltpu.make_async_copy(from_hbm[2].at[:, at], w_ref.at[:, at], sems.at[9 + i])
        )
        w_copies[-1].start()
    arrivals += [fetch(1)] + [fetch(i) for i in range(3, 9)]
    arrivals[0].wait()
    for i in range(parts):
        at = slice(i * part, (i + 1) * part)
        w_copies[i].wait()
        q_ref[:rows, at] = dot_f32(normed_refs[0][...], w_ref[:, at]).astype(BF16)
    arrivals[1].wait()
    q_ref[rows:, :] = dot_f32(normed_refs[1][...], w_ref[...]).astype(BF16)
    for copy in arrivals[2:]:
        copy.wait()
    for head in range(HEADS):
        at = columns(head)
        keys = [kv_ref[:, at] for kv_ref in own_and_near] + [far_k_ref[:, at]]
        values = [kv_ref[:, columns(HEADS + head)] for kv_ref in own_and_near] + [far_v_ref[:, at]]
        values = [with_ones(value) for value in values]
        for i, side in ((2, 0), (3, 0), (4, 1)):
            keys[i] = (keys[i].astype(F32) + embed_ref[side : side + 1, at]).astype(BF16)
        for block in range(2):
            here = slice(block * rows, (block + 1) * rows)
            query = q_ref[here, at]
            scores = [dot_nt(query, key) for key in keys]
            top = jnp.max(functools.reduce(jnp.maximum, scores), axis=-1, keepdims=True)
            acc = 0.0
            for score, value in zip(scores, values):
                acc = acc + dot_f32(jnp.exp2((score - top) * EXP2_SCALE).astype(BF16), value)
            acc_ref[here, at] = acc[:, :HEAD_DIM]
            total_ref[here, at] = acc[:, HEAD_DIM:]
            top_ref[here, at] = jnp.broadcast_to(top, (rows, HEAD_DIM))


def first_part(normed, w_query, embeds, own, near, far_key, far_value):
    rows = 2 * normed[0].shape[0]
    inner, width = w_query.shape[1], w_query.shape[0]
    wide = jax.ShapeDtypeStruct((rows, inner), F32)
    fetched = [*normed, w_query, *own, *near, far_key, far_value]
    return pl.pallas_call(
        first_kernel,
        in_specs=[VMEM] + [HBM] * len(fetched),
        out_specs=[VMEM] * 4,
        out_shape=[jax.ShapeDtypeStruct((rows, inner), BF16), wide, wide, wide],
        scratch_shapes=[pltpu.VMEM(array.shape, BF16) for array in fetched]
        + [pltpu.SemaphoreType.DMA((13,))],
        compiler_params=pltpu.CompilerParams(vmem_limit_bytes=24 * MIB),
        cost_estimate=pl.CostEstimate(flops=1, bytes_accessed=1, transcendentals=0),
        name="first_part",
    )(embeds, *in_hbm(*fetched))


def weigh_kernel(q_ref, acc_ref, top_ref, total_ref, key_ref, embed_ref, keep_ref, inverse_ref, weight_ref):
    half = key_ref.shape[0]
    for head in range(HEADS):
        at = columns(head)
        key = (key_ref[:, at].astype(F32) + embed_ref[1:2, at]).astype(BF16)
        for block in range(q_ref.shape[0] // half):
            here = slice(block * half, (block + 1) * half)
            scores = dot_nt(q_ref[here, at], key)
            before = top_ref[here, at]
            top = jnp.maximum(before, jnp.max(scores, axis=-1, keepdims=True))
            keep = jnp.exp2((before - top) * EXP2_SCALE)
            expo = jnp.exp2((scores - jnp.concatenate([top, top], axis=1)) * EXP2_SCALE).astype(BF16)
            weight_ref[here, head * half : (head + 1) * half] = expo
            total = dot_f32(expo, jnp.ones((half, HEAD_DIM), BF16)) + total_ref[here, at] * keep
            inverse_ref[here, at] = 1.0 / total
            keep_ref[here, at] = acc_ref[here, at] * keep


def weigh(query, acc, top, total, key, embeds):
    rows, inner = query.shape
    wide = jax.ShapeDtypeStruct((rows, inner), F32)
    return pl.pallas_call(
        weigh_kernel,
        in_specs=[VMEM] * 6,
        out_specs=[VMEM] * 3,
        out_shape=[wide, wide, jax.ShapeDtypeStruct((rows, HEADS * key.shape[0]), BF16)],
        compiler_params=pltpu.CompilerParams(vmem_limit_bytes=6 * MIB),
        cost_estimate=pl.CostEstimate(flops=1, bytes_accessed=1, transcendentals=0),
        name="weigh",
    )(query, acc, top, total, key, embeds)


def last_kernel(acc_ref, inverse_ref, weight_ref, piece_a_ref, piece_b_ref, stream_a_ref, stream_b_ref, w_ref, o_ref, out_ref):
    rows = stream_a_ref.shape[0]
    keys = piece_a_ref.shape[0]
    inner = HEADS * HEAD_DIM
    for block, stream_ref in enumerate((stream_a_ref, stream_b_ref)):
        here = slice(block * rows, (block + 1) * rows)
        for head in range(HEADS):
            at = columns(head)
            weights = weight_ref[here, head * keys : (head + 1) * keys]
            first = inner + head * HEAD_DIM
            value_at = slice(first, first + HEAD_DIM)
            value = alone_part((piece_a_ref, piece_b_ref), value_at, FIRST_PIECE)[...]
            acc = acc_ref[here, at] + dot_f32(weights, value)
            out_ref[here, at] = (acc * inverse_ref[here, at]).astype(BF16)
        product = dot_f32(out_ref[here, :], w_ref[...])
        o_ref[here, :] = (stream_ref[...].astype(F32) + product).astype(BF16)


def last_part(acc, inverse, weights, pieces, streams, w_out):
    inner, width = w_out.shape
    rows = acc.shape[0]
    return pl.pallas_call(
        last_kernel,
        in_specs=[VMEM] * 8,
        out_specs=VMEM,
        out_shape=jax.ShapeDtypeStruct((rows, width), BF16),
        scratch_shapes=[pltpu.VMEM((rows, inner), BF16)],
        compiler_params=pltpu.CompilerParams(vmem_limit_bytes=8 * MIB),
        cost_estimate=pl.CostEstimate(flops=1, bytes_accessed=1, transcendentals=0),
        name="last_part",
    )(acc, inverse, weights, *pieces, *streams, w_out)


def shards(
    hidden,
    t_query,
    t_key,
    t_value,
    frame_offsets,
    cycle_sides,
    w_temporal_out,
    norm_gain,
    w_query,
    w_key,
    w_value,
    w_cross_out,
    side_embed,
):
    rows_here = hidden.shape[2]
    model_width = hidden.shape[3]
    inner = t_query.shape[3]
    frames = lax.axis_size("frame")
    half = rows_here // 2
    group = half // frames
    hidden = hidden.reshape(rows_here, model_width)
    t_query = t_query.reshape(rows_here, inner)
    t_key = t_key.reshape(rows_here, inner)
    t_value = t_value.reshape(rows_here, inner)
    gain = norm_gain
    offsets = jnp.broadcast_to(frame_offsets.astype(F32)[:, None], (frames, HEAD_DIM))

    def exchange(value):
        return lax.all_to_all(value, "frame", split_axis=0, concat_axis=0, tiled=True)

    def to_near(value):
        return lax.ppermute(value, "cam", [(0, 1), (1, 0), (2, 3), (3, 2)])

    def to_far(value):
        return lax.ppermute(value, "cam", [(0, 3), (3, 0), (1, 2), (2, 1)])

    packed_a, cosine, sine = pack(t_query, t_key, t_value, offsets, rotary_frequencies())
    got_a = exchange(packed_a)
    weights = (w_temporal_out, gain, w_key, w_value)
    got_b = exchange(temporal(got_a, cosine, sine, group, [t_query, t_key, t_value]))
    stream_a, normed_a, kv_a, key_a, value_a = project_first(got_b, 3 * inner, hidden, *weights)
    far_key_a = to_far(key_a)
    far_key_a, value_a = lax.optimization_barrier((far_key_a, value_a))
    far_value_a = to_far(value_a)
    near_a = to_near(kv_a)
    got_b, key_a = lax.optimization_barrier((got_b, key_a))
    back_b = exchange(temporal(got_b, cosine, sine, group, []))
    stream_b, normed_b, kv_b, piece_b, rest_b = project_second(back_b, hidden, *weights)
    far_piece_b = to_far(piece_b)
    far_rest_b = to_far(rest_b)
    near_b = to_near(kv_b)
    token = side_embed[:, :HEAD_DIM]
    far_value_a, token = lax.optimization_barrier((far_value_a, token))
    token = to_near(token)
    token = to_near(token + 1)
    stream_b, cycle_sides, side_embed = lax.optimization_barrier((stream_b, cycle_sides, side_embed))
    near_cam = lax.axis_index("cam") ^ 1
    near_left = cycle_sides[0, 0] == near_cam
    side_f = side_embed.astype(F32)
    embeds = jnp.where(near_left, side_f, side_f[::-1])
    embeds, token = lax.optimization_barrier((embeds, token))
    embeds = embeds + 0.0 * token[:1, :1].astype(F32)
    query, acc, top, total = first_part(
        [normed_a, normed_b], w_query, embeds, [kv_a, kv_b], [near_a, near_b], far_key_a, far_value_a
    )
    acc, inverse, last_weights = weigh(query, acc, top, total, far_piece_b, embeds)
    mixed = last_part(acc, inverse, last_weights, [far_piece_b, far_rest_b], [stream_a, stream_b], w_cross_out)
    return mixed.reshape(1, 1, rows_here, model_width)


def solution(mesh):
    in_specs = (
        P("cam", "frame", None, None),
        P("cam", "frame", None, None),
        P("cam", "frame", None, None),
        P("cam", "frame", None, None),
        P(),
        P("cam", None),
        P(),
        P(),
        P(),
        P(),
        P(),
        P(),
        P(),
    )
    out_specs = P("cam", "frame", None, None)
    return jax.shard_map(shards, mesh=mesh, in_specs=in_specs, out_specs=out_specs, check_vma=False)
```

```python
import functools
import math

import jax
import jax.numpy as jnp
from jax import lax
from jax.experimental import pallas as pl
from jax.experimental.pallas import tpu as pltpu
from jax.sharding import PartitionSpec as P

HEADS = 8
HEAD_DIM = 128
MIB = 1 << 20
F32 = jnp.float32
BF16 = jnp.bfloat16
EXP2_SCALE = math.log2(math.e) / math.sqrt(HEAD_DIM)


def dot_f32(a, b):
    return jnp.dot(a, b, preferred_element_type=F32)


def dot_nt(a, b):
    return lax.dot_general(a, b, (((1,), (1,)), ((), ())), preferred_element_type=F32)


FIRST_PIECE = 1536
KV_CUTS = [slice(0, 512), slice(512, 1024), slice(1024, 1536), slice(1536, 2048)]


def alone_part(refs, at, split):
    second = at.start >= split
    first = at.start - split * second
    return refs[second].at[:, first : first + at.stop - at.start]


def rotary_frequencies():
    half_dim = HEAD_DIM // 2
    steps_f = jnp.arange(half_dim).astype(F32)
    frequencies = 10000.0 ** (-steps_f / half_dim)
    return jnp.concatenate([frequencies, frequencies])[None, :]


VMEM = pl.BlockSpec(memory_space=pltpu.VMEM)
HBM = pl.BlockSpec(memory_space=pltpu.HBM)


def columns(head):
    return slice(head * HEAD_DIM, (head + 1) * HEAD_DIM)


def with_ones(values):
    return jnp.concatenate([values, jnp.ones_like(values)], axis=1)


def copy_all(pairs, sems):
    copies = [pltpu.make_async_copy(a, b, sems.at[i]) for i, (a, b) in enumerate(pairs)]
    for copy in copies:
        copy.start()
    for copy in copies:
        copy.wait()


def in_hbm(*arrays):
    return [pltpu.with_memory_space_constraint(array, pltpu.HBM) for array in arrays]


def pack_kernel(q_ref, k_ref, v_ref, offset_ref, frequency_ref, o_ref, cos_ref, sin_ref, sems):
    rows, inner = o_ref.shape[0], q_ref.shape[1]
    moves = [
        pltpu.make_async_copy(ref.at[:rows, :], o_ref.at[:, i * inner : (i + 1) * inner], sems.at[i])
        for i, ref in enumerate((q_ref, k_ref, v_ref))
    ]
    for move in moves:
        move.start()
    frames = offset_ref.shape[0]
    group = rows // frames
    angles = offset_ref[...] * frequency_ref[...]
    lane = lax.broadcasted_iota(jnp.int32, angles.shape, 1)
    cosine = jnp.cos(angles)
    sine = jnp.sin(angles)
    sine = jnp.where(lane < HEAD_DIM // 2, -sine, sine)
    for frame in range(frames):
        at = slice(frame * group, (frame + 1) * group)
        cos_ref[at, :] = jnp.broadcast_to(cosine[frame : frame + 1, :], (group, HEAD_DIM))
        sin_ref[at, :] = jnp.broadcast_to(sine[frame : frame + 1, :], (group, HEAD_DIM))
    for move in moves:
        move.wait()


def pack(query, key, value, offsets, frequencies):
    rows, inner = query.shape
    half = rows // 2
    table = pltpu.VMEM((half, HEAD_DIM), F32)
    return pl.pallas_call(
        pack_kernel,
        in_specs=[HBM] * 3 + [VMEM] * 2,
        out_specs=[VMEM] * 3,
        out_shape=[pltpu.VMEM((half, 3 * inner), BF16), table, table],
        scratch_shapes=[pltpu.SemaphoreType.DMA((3,))],
        compiler_params=pltpu.CompilerParams(vmem_limit_bytes=4 * MIB),
        cost_estimate=pl.CostEstimate(flops=0, bytes_accessed=6 * rows * inner, transcendentals=0),
        name="pack",
    )(*in_hbm(query, key, value), offsets, frequencies)


def temporal_kernel(group, packed_ref, cos_ref, sin_ref, *refs):
    rows = packed_ref.shape[0]
    inner = HEADS * HEAD_DIM
    count = len(refs) - 3 if len(refs) > 3 else 0
    first = 0
    copies = []
    if not count:
        o_hbm, o_ref, sems = refs
    else:
        o_ref = refs[count]
        first = count * inner
        for i, ref in enumerate(refs[:count]):
            to = o_ref.at[:, i * inner : (i + 1) * inner]
            copies.append(pltpu.make_async_copy(ref.at[rows:, :], to, refs[count + 2].at[i]))
            copies[-1].start()
    cosine = cos_ref[...]
    sine = sin_ref[...]
    row_at = lax.broadcasted_iota(jnp.int32, (rows, rows), 0)
    key_at = lax.broadcasted_iota(jnp.int32, (rows, rows), 1)
    same = lax.rem(row_at, group) == lax.rem(key_at, group)
    def rotated(part):
        part = part.astype(F32)
        return (part * cosine + pltpu.roll(part, HEAD_DIM // 2, 1) * sine).astype(BF16)

    for head in range(HEADS):
        query = rotated(packed_ref[:, columns(head)])
        key = rotated(packed_ref[:, columns(HEADS + head)])
        value = packed_ref[:, columns(2 * HEADS + head)]
        scores = jnp.where(same, dot_nt(query, key), -jnp.inf)
        top = jnp.max(scores, axis=-1, keepdims=True)
        expo = jnp.exp2((scores - top) * EXP2_SCALE).astype(BF16)
        both = dot_f32(expo, with_ones(value))
        result = both[:, :HEAD_DIM] / both[:, HEAD_DIM:]
        o_ref[:, first + head * HEAD_DIM : first + (head + 1) * HEAD_DIM] = result.astype(BF16)
        if not count and head % 2 == 1:
            at = slice((head - 1) * HEAD_DIM, (head + 1) * HEAD_DIM)
            copies.append(pltpu.make_async_copy(o_ref.at[:, at], o_hbm.at[:, at], sems.at[head // 2]))
            copies[-1].start()
    for copy in copies:
        copy.wait()


def temporal(packed, cosine, sine, group, following):
    rows = packed.shape[0]
    inner = HEADS * HEAD_DIM
    count = len(following)
    shape = (rows, inner * (1 + count))
    return pl.pallas_call(
        functools.partial(temporal_kernel, group),
        in_specs=[VMEM] * 3 + [HBM] * count,
        out_specs=VMEM if count else HBM,
        out_shape=jax.ShapeDtypeStruct(shape, BF16) if count else pltpu.HBM(shape, BF16),
        scratch_shapes=[pltpu.VMEM((8, 128) if count else shape, BF16), pltpu.SemaphoreType.DMA((4,))],
        compiler_params=pltpu.CompilerParams(vmem_limit_bytes=6 * MIB),
        cost_estimate=pl.CostEstimate(
            flops=20_000_000_000 if count else 1, bytes_accessed=1, transcendentals=0
        ),
        name="temporal",
    )(packed, cosine, sine, *in_hbm(*following))


def project_rows(t_ref, hidden, w_out_ref, gain_ref, w_key_ref, w_value_ref, stream_ref, normed_ref, kv_ref, ready, done):
    inner, width = w_out_ref.shape
    part = 512
    squares = 0.0
    for i in range(width // part):
        at = slice(i * part, (i + 1) * part)
        ready(i)
        stream = (hidden[:, at].astype(F32) + dot_f32(t_ref[...], w_out_ref[:, at])).astype(BF16)
        stream_ref[:, at] = stream
        stream = stream.astype(F32)
        squares = squares + jnp.sum(stream * stream, axis=-1, keepdims=True)
    done(0)
    scale = lax.rsqrt(squares / width + 1e-06)
    normed_ref[...] = (stream_ref[...].astype(F32) * scale * gain_ref[...].astype(F32).reshape(1, width)).astype(BF16)
    done(1)
    for i, at in enumerate(KV_CUTS):
        ready(width // part + i)
        w_ref = w_key_ref if at.start < inner else w_value_ref
        from_w = slice(at.start % inner, at.start % inner + at.stop - at.start)
        kv_ref[:, at] = dot_f32(normed_ref[...], w_ref[:, from_w]).astype(BF16)
        done(2 + i)


def project_first_kernel(t_at, t_ref, hidden_ref, w_out_ref, gain_ref, w_key_ref, w_value_ref, *refs):
    outs, alone, scratch, sems = refs[:3], refs[3:5], refs[5:8], refs[8]
    rows = t_ref.shape[0]
    inner = w_out_ref.shape[0]
    copies = []

    def leave(a, b):
        copies.append(pltpu.make_async_copy(a, b, sems.at[len(copies)]))
        copies[-1].start()

    def done(i):
        if i < 2:
            leave(scratch[i], outs[i])
        else:
            at = KV_CUTS[i - 2]
            leave(scratch[2].at[:, at], alone_part(alone, at, inner))
            leave(scratch[2].at[:, at], outs[2].at[:, at])

    project_rows(
        t_ref.at[:, t_at : t_at + inner],
        hidden_ref.at[:rows, :],
        w_out_ref,
        gain_ref,
        w_key_ref,
        w_value_ref,
        *scratch,
        lambda i: None,
        done,
    )
    for copy in copies:
        copy.wait()


def project_first(t_out, t_at, hidden, w_out, gain, w_key, w_value):
    rows = t_out.shape[0]
    inner = HEADS * HEAD_DIM
    width = hidden.shape[1]
    shapes = [(rows, width), (rows, width), (rows, 2 * inner)]
    return pl.pallas_call(
        functools.partial(project_first_kernel, t_at),
        in_specs=[VMEM] * 6,
        out_specs=[HBM] * 5,
        out_shape=[pltpu.HBM(shape, BF16) for shape in shapes + [(rows, inner)] * 2],
        scratch_shapes=[pltpu.VMEM(shape, BF16) for shape in shapes]
        + [pltpu.SemaphoreType.DMA((12,))],
        compiler_params=pltpu.CompilerParams(vmem_limit_bytes=10 * MIB),
        cost_estimate=pl.CostEstimate(flops=1, bytes_accessed=1, transcendentals=0),
        name="project_first",
    )(t_out, hidden, w_out, gain, w_key, w_value)


def project_second_kernel(t_ref, gain_ref, hidden_hbm, *refs):
    w_hbm, outs, alone, hidden_ref, normed_ref, kv_ref = refs[:3], refs[3:6], refs[6:8], *refs[8:11]
    w_refs, arrived, left = refs[11:14], refs[14], refs[15]
    rows = t_ref.shape[0]
    inner = HEADS * HEAD_DIM
    part = 512
    get_hidden = pltpu.make_async_copy(hidden_hbm.at[rows:, :], hidden_ref, arrived.at[9])
    get_hidden.start()
    cuts = [(0, slice(i, i + part)) for i in range(0, w_hbm[0].shape[1], part)]
    for at in KV_CUTS:
        first = at.start % inner
        cuts.append((1 + at.start // inner, slice(first, first + at.stop - at.start)))
    copies = []
    for i, (which, at) in enumerate(cuts):
        copies.append(
            pltpu.make_async_copy(w_hbm[which].at[:, at], w_refs[which].at[:, at], arrived.at[i])
        )
        copies[-1].start()
    leaving = []

    def leave(a, b):
        leaving.append(pltpu.make_async_copy(a, b, left.at[len(leaving)]))
        leaving[-1].start()

    def done(i):
        if i == 1:
            leave(normed_ref, outs[1])
        if i >= 2:
            at = KV_CUTS[i - 2]
            leave(kv_ref.at[:, at], alone_part(alone, at, FIRST_PIECE))
            leave(kv_ref.at[:, at], outs[2].at[:, at])

    get_hidden.wait()
    project_rows(
        t_ref,
        hidden_ref,
        w_refs[0],
        gain_ref,
        w_refs[1],
        w_refs[2],
        outs[0],
        normed_ref,
        kv_ref,
        lambda i: copies[i].wait(),
        done,
    )
    for copy in leaving:
        copy.wait()


def project_second(t_out, hidden, w_out, gain, w_key, w_value):
    rows = t_out.shape[0]
    inner = HEADS * HEAD_DIM
    width = hidden.shape[1]
    shapes = [(rows, width), (rows, width), (rows, 2 * inner)]
    weights = (w_out, w_key, w_value)
    return pl.pallas_call(
        project_second_kernel,
        in_specs=[VMEM] * 2 + [HBM] * 4,
        out_specs=[VMEM] + [HBM] * 4,
        out_shape=[jax.ShapeDtypeStruct(shapes[0], BF16)]
        + [
            pltpu.HBM(shape, BF16)
            for shape in shapes[1:] + [(rows, FIRST_PIECE), (rows, 2 * inner - FIRST_PIECE)]
        ],
        scratch_shapes=[pltpu.VMEM((rows, width), BF16)]
        + [pltpu.VMEM(shape, BF16) for shape in shapes[1:]]
        + [pltpu.VMEM(w.shape, BF16) for w in weights]
        + [pltpu.SemaphoreType.DMA((10,)), pltpu.SemaphoreType.DMA((11,))],
        compiler_params=pltpu.CompilerParams(vmem_limit_bytes=24 * MIB),
        cost_estimate=pl.CostEstimate(flops=1, bytes_accessed=1, transcendentals=0),
        name="project_second",
    )(t_out, gain, *in_hbm(hidden, *weights))


def first_kernel(embed_ref, *refs):
    from_hbm, (q_ref, acc_ref, top_ref, total_ref), held, sems = refs[:9], refs[9:13], refs[13:22], refs[22]
    normed_refs, w_ref, own_and_near, (far_k_ref, far_v_ref) = held[:2], held[2], held[3:7], held[7:9]
    rows = normed_refs[0].shape[0]
    part = 256
    parts = w_ref.shape[1] // part

    def fetch(i):
        copy = pltpu.make_async_copy(from_hbm[i], held[i], sems.at[i])
        copy.start()
        return copy

    w_copies = []
    arrivals = [fetch(0)]
    for i in range(parts):
        at = slice(i * part, (i + 1) * part)
        w_copies.append(
            pltpu.make_async_copy(from_hbm[2].at[:, at], w_ref.at[:, at], sems.at[9 + i])
        )
        w_copies[-1].start()
    arrivals += [fetch(1)] + [fetch(i) for i in range(3, 9)]
    arrivals[0].wait()
    for i in range(parts):
        at = slice(i * part, (i + 1) * part)
        w_copies[i].wait()
        q_ref[:rows, at] = dot_f32(normed_refs[0][...], w_ref[:, at]).astype(BF16)
    arrivals[1].wait()
    q_ref[rows:, :] = dot_f32(normed_refs[1][...], w_ref[...]).astype(BF16)
    for copy in arrivals[2:]:
        copy.wait()
    for head in range(HEADS):
        at = columns(head)
        keys = [kv_ref[:, at] for kv_ref in own_and_near] + [far_k_ref[:, at]]
        values = [kv_ref[:, columns(HEADS + head)] for kv_ref in own_and_near] + [far_v_ref[:, at]]
        values = [with_ones(value) for value in values]
        for i, side in ((2, 0), (3, 0), (4, 1)):
            keys[i] = (keys[i].astype(F32) + embed_ref[side : side + 1, at]).astype(BF16)
        for block in range(2):
            here = slice(block * rows, (block + 1) * rows)
            query = q_ref[here, at]
            scores = [dot_nt(query, key) for key in keys]
            top = jnp.max(functools.reduce(jnp.maximum, scores), axis=-1, keepdims=True)
            acc = 0.0
            for score, value in zip(scores, values):
                acc = acc + dot_f32(jnp.exp2((score - top) * EXP2_SCALE).astype(BF16), value)
            acc_ref[here, at] = acc[:, :HEAD_DIM]
            total_ref[here, at] = acc[:, HEAD_DIM:]
            top_ref[here, at] = jnp.broadcast_to(top, (rows, HEAD_DIM))


def first_part(normed, w_query, embeds, own, near, far_key, far_value):
    rows = 2 * normed[0].shape[0]
    inner, width = w_query.shape[1], w_query.shape[0]
    wide = jax.ShapeDtypeStruct((rows, inner), F32)
    fetched = [*normed, w_query, *own, *near, far_key, far_value]
    return pl.pallas_call(
        first_kernel,
        in_specs=[VMEM] + [HBM] * len(fetched),
        out_specs=[VMEM] * 4,
        out_shape=[jax.ShapeDtypeStruct((rows, inner), BF16), wide, wide, wide],
        scratch_shapes=[pltpu.VMEM(array.shape, BF16) for array in fetched]
        + [pltpu.SemaphoreType.DMA((13,))],
        compiler_params=pltpu.CompilerParams(vmem_limit_bytes=24 * MIB),
        cost_estimate=pl.CostEstimate(flops=1, bytes_accessed=1, transcendentals=0),
        name="first_part",
    )(embeds, *in_hbm(*fetched))


def weigh_kernel(q_ref, acc_ref, top_ref, total_ref, key_ref, embed_ref, keep_ref, inverse_ref, weight_ref):
    half = key_ref.shape[0]
    for head in range(HEADS):
        at = columns(head)
        key = (key_ref[:, at].astype(F32) + embed_ref[1:2, at]).astype(BF16)
        for block in range(q_ref.shape[0] // half):
            here = slice(block * half, (block + 1) * half)
            scores = dot_nt(q_ref[here, at], key)
            before = top_ref[here, at]
            top = jnp.maximum(before, jnp.max(scores, axis=-1, keepdims=True))
            keep = jnp.exp2((before - top) * EXP2_SCALE)
            expo = jnp.exp2((scores - jnp.concatenate([top, top], axis=1)) * EXP2_SCALE).astype(BF16)
            weight_ref[here, head * half : (head + 1) * half] = expo
            total = dot_f32(expo, jnp.ones((half, HEAD_DIM), BF16)) + total_ref[here, at] * keep
            inverse_ref[here, at] = 1.0 / total
            keep_ref[here, at] = acc_ref[here, at] * keep


def weigh(query, acc, top, total, key, embeds):
    rows, inner = query.shape
    wide = jax.ShapeDtypeStruct((rows, inner), F32)
    return pl.pallas_call(
        weigh_kernel,
        in_specs=[VMEM] * 6,
        out_specs=[VMEM] * 3,
        out_shape=[wide, wide, jax.ShapeDtypeStruct((rows, HEADS * key.shape[0]), BF16)],
        compiler_params=pltpu.CompilerParams(vmem_limit_bytes=6 * MIB),
        cost_estimate=pl.CostEstimate(flops=1, bytes_accessed=1, transcendentals=0),
        name="weigh",
    )(query, acc, top, total, key, embeds)


def last_kernel(acc_ref, inverse_ref, weight_ref, piece_a_ref, piece_b_ref, stream_a_ref, stream_b_ref, w_ref, o_hbm, out_ref, o_ref, sems):
    rows = stream_a_ref.shape[0]
    keys = piece_a_ref.shape[0]
    inner = HEADS * HEAD_DIM
    copies = []
    for block, stream_ref in enumerate((stream_a_ref, stream_b_ref)):
        here = slice(block * rows, (block + 1) * rows)
        for head in range(HEADS):
            at = columns(head)
            weights = weight_ref[here, head * keys : (head + 1) * keys]
            first = inner + head * HEAD_DIM
            value_at = slice(first, first + HEAD_DIM)
            value = alone_part((piece_a_ref, piece_b_ref), value_at, FIRST_PIECE)[...]
            acc = acc_ref[here, at] + dot_f32(weights, value)
            out_ref[here, at] = (acc * inverse_ref[here, at]).astype(BF16)
        for i in range(4):
            cols = slice(i * 512, (i + 1) * 512)
            product = dot_f32(out_ref[here, :], w_ref[:, cols])
            o_ref[here, cols] = (stream_ref[:, cols].astype(F32) + product).astype(BF16)
            copies.append(
                pltpu.make_async_copy(
                    o_ref.at[here, cols], o_hbm.at[here, cols], sems.at[len(copies)]
                )
            )
            copies[-1].start()
    for copy in copies:
        copy.wait()


def last_part(acc, inverse, weights, pieces, streams, w_out):
    inner, width = w_out.shape
    rows = acc.shape[0]
    return pl.pallas_call(
        last_kernel,
        in_specs=[VMEM] * 8,
        out_specs=HBM,
        out_shape=pltpu.HBM((rows, width), BF16),
        scratch_shapes=[
            pltpu.VMEM((rows, inner), BF16),
            pltpu.VMEM((rows, width), BF16),
            pltpu.SemaphoreType.DMA((8,)),
        ],
        compiler_params=pltpu.CompilerParams(vmem_limit_bytes=8 * MIB),
        cost_estimate=pl.CostEstimate(flops=1, bytes_accessed=1, transcendentals=0),
        name="last_part",
    )(acc, inverse, weights, *pieces, *streams, w_out)


def shards(
    hidden,
    t_query,
    t_key,
    t_value,
    frame_offsets,
    cycle_sides,
    w_temporal_out,
    norm_gain,
    w_query,
    w_key,
    w_value,
    w_cross_out,
    side_embed,
):
    rows_here = hidden.shape[2]
    model_width = hidden.shape[3]
    inner = t_query.shape[3]
    frames = lax.axis_size("frame")
    half = rows_here // 2
    group = half // frames
    hidden = hidden.reshape(rows_here, model_width)
    t_query = t_query.reshape(rows_here, inner)
    t_key = t_key.reshape(rows_here, inner)
    t_value = t_value.reshape(rows_here, inner)
    gain = norm_gain
    offsets = jnp.broadcast_to(frame_offsets.astype(F32)[:, None], (frames, HEAD_DIM))

    def exchange(value):
        return lax.all_to_all(value, "frame", split_axis=0, concat_axis=0, tiled=True)

    def to_near(value):
        return lax.ppermute(value, "cam", [(0, 1), (1, 0), (2, 3), (3, 2)])

    def to_far(value):
        return lax.ppermute(value, "cam", [(0, 3), (3, 0), (1, 2), (2, 1)])

    packed_a, cosine, sine = pack(t_query, t_key, t_value, offsets, rotary_frequencies())
    got_a = exchange(packed_a)
    weights = (w_temporal_out, gain, w_key, w_value)
    got_b = exchange(temporal(got_a, cosine, sine, group, [t_query, t_key, t_value]))
    stream_a, normed_a, kv_a, key_a, value_a = project_first(got_b, 3 * inner, hidden, *weights)
    far_key_a = to_far(key_a)
    far_key_a, value_a = lax.optimization_barrier((far_key_a, value_a))
    far_value_a = to_far(value_a)
    near_a = to_near(kv_a)
    got_b, key_a = lax.optimization_barrier((got_b, key_a))
    back_b = exchange(temporal(got_b, cosine, sine, group, []))
    stream_b, normed_b, kv_b, piece_b, rest_b = project_second(back_b, hidden, *weights)
    far_piece_b = to_far(piece_b)
    far_rest_b = to_far(rest_b)
    near_b = to_near(kv_b)
    token = side_embed[:, :HEAD_DIM]
    far_value_a, token = lax.optimization_barrier((far_value_a, token))
    token = to_near(token)
    token = to_near(token + 1)
    stream_b, cycle_sides, side_embed = lax.optimization_barrier((stream_b, cycle_sides, side_embed))
    near_cam = lax.axis_index("cam") ^ 1
    near_left = cycle_sides[0, 0] == near_cam
    side_f = side_embed.astype(F32)
    embeds = jnp.where(near_left, side_f, side_f[::-1])
    embeds, token = lax.optimization_barrier((embeds, token))
    embeds = embeds + 0.0 * token[:1, :1].astype(F32)
    query, acc, top, total = first_part(
        [normed_a, normed_b], w_query, embeds, [kv_a, kv_b], [near_a, near_b], far_key_a, far_value_a
    )
    acc, inverse, last_weights = weigh(query, acc, top, total, far_piece_b, embeds)
    mixed = last_part(acc, inverse, last_weights, [far_piece_b, far_rest_b], [stream_a, stream_b], w_cross_out)
    return mixed.reshape(1, 1, rows_here, model_width)


def solution(mesh):
    in_specs = (
        P("cam", "frame", None, None),
        P("cam", "frame", None, None),
        P("cam", "frame", None, None),
        P("cam", "frame", None, None),
        P(),
        P("cam", None),
        P(),
        P(),
        P(),
        P(),
        P(),
        P(),
        P(),
    )
    out_specs = P("cam", "frame", None, None)
    return jax.shard_map(shards, mesh=mesh, in_specs=in_specs, out_specs=out_specs, check_vma=False)
```

```python
import functools
import math

import jax
import jax.numpy as jnp
from jax import lax
from jax.experimental import pallas as pl
from jax.experimental.pallas import tpu as pltpu
from jax.sharding import PartitionSpec as P

HEADS = 8
HEAD_DIM = 128
MIB = 1 << 20
F32 = jnp.float32
BF16 = jnp.bfloat16
EXP2_SCALE = math.log2(math.e) / math.sqrt(HEAD_DIM)


def dot_f32(a, b):
    return jnp.dot(a, b, preferred_element_type=F32)


def dot_nt(a, b):
    return lax.dot_general(a, b, (((1,), (1,)), ((), ())), preferred_element_type=F32)


FIRST_PIECE = 1536
KV_CUTS = [slice(0, 512), slice(512, 1024), slice(1024, 1536), slice(1536, 2048)]


def alone_part(refs, at, split):
    second = at.start >= split
    first = at.start - split * second
    return refs[second].at[:, first : first + at.stop - at.start]


def rotary_frequencies():
    half_dim = HEAD_DIM // 2
    steps_f = jnp.arange(half_dim).astype(F32)
    frequencies = 10000.0 ** (-steps_f / half_dim)
    return jnp.concatenate([frequencies, frequencies])[None, :]


VMEM = pl.BlockSpec(memory_space=pltpu.VMEM)
HBM = pl.BlockSpec(memory_space=pltpu.HBM)


def columns(head):
    return slice(head * HEAD_DIM, (head + 1) * HEAD_DIM)


def with_ones(values):
    return jnp.concatenate([values, jnp.ones_like(values)], axis=1)


def copy_all(pairs, sems):
    copies = [pltpu.make_async_copy(a, b, sems.at[i]) for i, (a, b) in enumerate(pairs)]
    for copy in copies:
        copy.start()
    for copy in copies:
        copy.wait()


def in_hbm(*arrays):
    return [pltpu.with_memory_space_constraint(array, pltpu.HBM) for array in arrays]


def pack_kernel(q_ref, k_ref, v_ref, offset_ref, frequency_ref, o_ref, cos_ref, sin_ref, sems):
    rows, inner = o_ref.shape[0], q_ref.shape[1]
    moves = [
        pltpu.make_async_copy(ref.at[:rows, :], o_ref.at[:, i * inner : (i + 1) * inner], sems.at[i])
        for i, ref in enumerate((q_ref, k_ref, v_ref))
    ]
    for move in moves:
        move.start()
    frames = offset_ref.shape[0]
    group = rows // frames
    angles = offset_ref[...] * frequency_ref[...]
    lane = lax.broadcasted_iota(jnp.int32, angles.shape, 1)
    cosine = jnp.cos(angles)
    sine = jnp.sin(angles)
    sine = jnp.where(lane < HEAD_DIM // 2, -sine, sine)
    for frame in range(frames):
        at = slice(frame * group, (frame + 1) * group)
        cos_ref[at, :] = jnp.broadcast_to(cosine[frame : frame + 1, :], (group, HEAD_DIM))
        sin_ref[at, :] = jnp.broadcast_to(sine[frame : frame + 1, :], (group, HEAD_DIM))
    for move in moves:
        move.wait()


def pack(query, key, value, offsets, frequencies):
    rows, inner = query.shape
    half = rows // 2
    table = pltpu.VMEM((half, HEAD_DIM), F32)
    return pl.pallas_call(
        pack_kernel,
        in_specs=[HBM] * 3 + [VMEM] * 2,
        out_specs=[VMEM] * 3,
        out_shape=[pltpu.VMEM((half, 3 * inner), BF16), table, table],
        scratch_shapes=[pltpu.SemaphoreType.DMA((3,))],
        compiler_params=pltpu.CompilerParams(vmem_limit_bytes=4 * MIB),
        cost_estimate=pl.CostEstimate(flops=0, bytes_accessed=6 * rows * inner, transcendentals=0),
        name="pack",
    )(*in_hbm(query, key, value), offsets, frequencies)


def temporal_kernel(group, packed_ref, cos_ref, sin_ref, *refs):
    rows = packed_ref.shape[0]
    inner = HEADS * HEAD_DIM
    count = len(refs) - 3 if len(refs) > 3 else 0
    first = 0
    copies = []
    if not count:
        o_hbm, o_ref, sems = refs
    else:
        o_ref = refs[count]
        first = count * inner
        for i, ref in enumerate(refs[:count]):
            to = o_ref.at[:, i * inner : (i + 1) * inner]
            copies.append(pltpu.make_async_copy(ref.at[rows:, :], to, refs[count + 2].at[i]))
            copies[-1].start()
    cosine = cos_ref[...]
    sine = sin_ref[...]
    row_at = lax.broadcasted_iota(jnp.int32, (rows, rows), 0)
    key_at = lax.broadcasted_iota(jnp.int32, (rows, rows), 1)
    same = lax.rem(row_at, group) == lax.rem(key_at, group)
    def rotated(part):
        part = part.astype(F32)
        return (part * cosine + pltpu.roll(part, HEAD_DIM // 2, 1) * sine).astype(BF16)

    for head in range(HEADS):
        query = rotated(packed_ref[:, columns(head)])
        key = rotated(packed_ref[:, columns(HEADS + head)])
        value = packed_ref[:, columns(2 * HEADS + head)]
        scores = jnp.where(same, dot_nt(query, key), -jnp.inf)
        top = jnp.max(scores, axis=-1, keepdims=True)
        expo = jnp.exp2((scores - top) * EXP2_SCALE).astype(BF16)
        both = dot_f32(expo, with_ones(value))
        result = both[:, :HEAD_DIM] / both[:, HEAD_DIM:]
        o_ref[:, first + head * HEAD_DIM : first + (head + 1) * HEAD_DIM] = result.astype(BF16)
        if not count and head % 2 == 1:
            at = slice((head - 1) * HEAD_DIM, (head + 1) * HEAD_DIM)
            copies.append(pltpu.make_async_copy(o_ref.at[:, at], o_hbm.at[:, at], sems.at[head // 2]))
            copies[-1].start()
    for copy in copies:
        copy.wait()


def temporal(packed, cosine, sine, group, following):
    rows = packed.shape[0]
    inner = HEADS * HEAD_DIM
    count = len(following)
    shape = (rows, inner * (1 + count))
    return pl.pallas_call(
        functools.partial(temporal_kernel, group),
        in_specs=[VMEM] * 3 + [HBM] * count,
        out_specs=VMEM if count else HBM,
        out_shape=jax.ShapeDtypeStruct(shape, BF16) if count else pltpu.HBM(shape, BF16),
        scratch_shapes=[pltpu.VMEM((8, 128) if count else shape, BF16), pltpu.SemaphoreType.DMA((4,))],
        compiler_params=pltpu.CompilerParams(vmem_limit_bytes=6 * MIB),
        cost_estimate=pl.CostEstimate(
            flops=20_000_000_000 if count else 1, bytes_accessed=1, transcendentals=0
        ),
        name="temporal",
    )(packed, cosine, sine, *in_hbm(*following))


def project_rows(t_ref, hidden, w_out_ref, gain_ref, w_key_ref, w_value_ref, stream_ref, normed_ref, kv_ref, ready, done):
    inner, width = w_out_ref.shape
    part = 512
    squares = 0.0
    for i in range(width // part):
        at = slice(i * part, (i + 1) * part)
        ready(i)
        stream = (hidden[:, at].astype(F32) + dot_f32(t_ref[...], w_out_ref[:, at])).astype(BF16)
        stream_ref[:, at] = stream
        stream = stream.astype(F32)
        squares = squares + jnp.sum(stream * stream, axis=-1, keepdims=True)
    done(0)
    scale = lax.rsqrt(squares / width + 1e-06)
    normed_ref[...] = (stream_ref[...].astype(F32) * scale * gain_ref[...].astype(F32).reshape(1, width)).astype(BF16)
    done(1)
    for i, at in enumerate(KV_CUTS):
        ready(width // part + i)
        w_ref = w_key_ref if at.start < inner else w_value_ref
        from_w = slice(at.start % inner, at.start % inner + at.stop - at.start)
        kv_ref[:, at] = dot_f32(normed_ref[...], w_ref[:, from_w]).astype(BF16)
        done(2 + i)


def project_first_kernel(t_at, t_ref, hidden_ref, w_out_ref, gain_ref, w_key_ref, w_value_ref, *refs):
    outs, alone, scratch, sems = refs[:3], refs[3:5], refs[5:8], refs[8]
    rows = t_ref.shape[0]
    inner = w_out_ref.shape[0]
    copies = []

    def leave(a, b):
        copies.append(pltpu.make_async_copy(a, b, sems.at[len(copies)]))
        copies[-1].start()

    def done(i):
        if i < 2:
            leave(scratch[i], outs[i])
        else:
            at = KV_CUTS[i - 2]
            leave(scratch[2].at[:, at], alone_part(alone, at, inner))
            leave(scratch[2].at[:, at], outs[2].at[:, at])

    project_rows(
        t_ref.at[:, t_at : t_at + inner],
        hidden_ref.at[:rows, :],
        w_out_ref,
        gain_ref,
        w_key_ref,
        w_value_ref,
        *scratch,
        lambda i: None,
        done,
    )
    for copy in copies:
        copy.wait()


def project_first(t_out, t_at, hidden, w_out, gain, w_key, w_value):
    rows = t_out.shape[0]
    inner = HEADS * HEAD_DIM
    width = hidden.shape[1]
    shapes = [(rows, width), (rows, width), (rows, 2 * inner)]
    return pl.pallas_call(
        functools.partial(project_first_kernel, t_at),
        in_specs=[VMEM] * 6,
        out_specs=[HBM] * 5,
        out_shape=[pltpu.HBM(shape, BF16) for shape in shapes + [(rows, inner)] * 2],
        scratch_shapes=[pltpu.VMEM(shape, BF16) for shape in shapes]
        + [pltpu.SemaphoreType.DMA((12,))],
        compiler_params=pltpu.CompilerParams(vmem_limit_bytes=10 * MIB),
        cost_estimate=pl.CostEstimate(flops=1, bytes_accessed=1, transcendentals=0),
        name="project_first",
    )(t_out, hidden, w_out, gain, w_key, w_value)


def project_second_kernel(t_ref, gain_ref, hidden_hbm, *refs):
    w_hbm, outs, alone, hidden_ref, normed_ref, kv_ref = refs[:3], refs[3:6], refs[6:8], *refs[8:11]
    w_refs, arrived, left = refs[11:14], refs[14], refs[15]
    rows = t_ref.shape[0]
    inner = HEADS * HEAD_DIM
    part = 512
    get_hidden = pltpu.make_async_copy(hidden_hbm.at[rows:, :], hidden_ref, arrived.at[9])
    get_hidden.start()
    copies = [
        pltpu.make_async_copy(a, b, arrived.at[i]) for i, (a, b) in enumerate(zip(w_hbm, w_refs))
    ]
    for copy in copies:
        copy.start()
    first_use = {0: 0, w_hbm[0].shape[1] // part: 1, w_hbm[0].shape[1] // part + inner // part: 2}

    def ready(i):
        if i in first_use:
            copies[first_use[i]].wait()

    leaving = []

    def leave(a, b):
        leaving.append(pltpu.make_async_copy(a, b, left.at[len(leaving)]))
        leaving[-1].start()

    def done(i):
        if i == 1:
            leave(normed_ref, outs[1])
        if i >= 2:
            at = KV_CUTS[i - 2]
            leave(kv_ref.at[:, at], alone_part(alone, at, FIRST_PIECE))
            leave(kv_ref.at[:, at], outs[2].at[:, at])

    get_hidden.wait()
    project_rows(
        t_ref,
        hidden_ref,
        w_refs[0],
        gain_ref,
        w_refs[1],
        w_refs[2],
        outs[0],
        normed_ref,
        kv_ref,
        ready,
        done,
    )
    for copy in leaving:
        copy.wait()


def project_second(t_out, hidden, w_out, gain, w_key, w_value):
    rows = t_out.shape[0]
    inner = HEADS * HEAD_DIM
    width = hidden.shape[1]
    shapes = [(rows, width), (rows, width), (rows, 2 * inner)]
    weights = (w_out, w_key, w_value)
    return pl.pallas_call(
        project_second_kernel,
        in_specs=[VMEM] * 2 + [HBM] * 4,
        out_specs=[VMEM] + [HBM] * 4,
        out_shape=[jax.ShapeDtypeStruct(shapes[0], BF16)]
        + [
            pltpu.HBM(shape, BF16)
            for shape in shapes[1:] + [(rows, FIRST_PIECE), (rows, 2 * inner - FIRST_PIECE)]
        ],
        scratch_shapes=[pltpu.VMEM((rows, width), BF16)]
        + [pltpu.VMEM(shape, BF16) for shape in shapes[1:]]
        + [pltpu.VMEM(w.shape, BF16) for w in weights]
        + [pltpu.SemaphoreType.DMA((10,)), pltpu.SemaphoreType.DMA((11,))],
        compiler_params=pltpu.CompilerParams(vmem_limit_bytes=24 * MIB),
        cost_estimate=pl.CostEstimate(flops=1, bytes_accessed=1, transcendentals=0),
        name="project_second",
    )(t_out, gain, *in_hbm(hidden, *weights))


def first_kernel(embed_ref, *refs):
    from_hbm, (q_ref, acc_ref, top_ref, total_ref), held, sems = refs[:9], refs[9:13], refs[13:22], refs[22]
    normed_refs, w_ref, own_and_near, (far_k_ref, far_v_ref) = held[:2], held[2], held[3:7], held[7:9]
    rows = normed_refs[0].shape[0]
    part = 256
    parts = w_ref.shape[1] // part

    def fetch(i):
        copy = pltpu.make_async_copy(from_hbm[i], held[i], sems.at[i])
        copy.start()
        return copy

    w_copies = []
    arrivals = [fetch(0)]
    for i in range(parts):
        at = slice(i * part, (i + 1) * part)
        w_copies.append(
            pltpu.make_async_copy(from_hbm[2].at[:, at], w_ref.at[:, at], sems.at[9 + i])
        )
        w_copies[-1].start()
    arrivals += [fetch(1)] + [fetch(i) for i in range(3, 9)]
    arrivals[0].wait()
    for i in range(parts):
        at = slice(i * part, (i + 1) * part)
        w_copies[i].wait()
        q_ref[:rows, at] = dot_f32(normed_refs[0][...], w_ref[:, at]).astype(BF16)
    arrivals[1].wait()
    q_ref[rows:, :] = dot_f32(normed_refs[1][...], w_ref[...]).astype(BF16)
    for copy in arrivals[2:]:
        copy.wait()
    for head in range(HEADS):
        at = columns(head)
        keys = [kv_ref[:, at] for kv_ref in own_and_near] + [far_k_ref[:, at]]
        values = [kv_ref[:, columns(HEADS + head)] for kv_ref in own_and_near] + [far_v_ref[:, at]]
        values = [with_ones(value) for value in values]
        for i, side in ((2, 0), (3, 0), (4, 1)):
            keys[i] = (keys[i].astype(F32) + embed_ref[side : side + 1, at]).astype(BF16)
        for block in range(2):
            here = slice(block * rows, (block + 1) * rows)
            query = q_ref[here, at]
            scores = [dot_nt(query, key) for key in keys]
            top = jnp.max(functools.reduce(jnp.maximum, scores), axis=-1, keepdims=True)
            acc = 0.0
            for score, value in zip(scores, values):
                acc = acc + dot_f32(jnp.exp2((score - top) * EXP2_SCALE).astype(BF16), value)
            acc_ref[here, at] = acc[:, :HEAD_DIM]
            total_ref[here, at] = acc[:, HEAD_DIM:]
            top_ref[here, at] = jnp.broadcast_to(top, (rows, HEAD_DIM))


def first_part(normed, w_query, embeds, own, near, far_key, far_value):
    rows = 2 * normed[0].shape[0]
    inner, width = w_query.shape[1], w_query.shape[0]
    wide = jax.ShapeDtypeStruct((rows, inner), F32)
    fetched = [*normed, w_query, *own, *near, far_key, far_value]
    return pl.pallas_call(
        first_kernel,
        in_specs=[VMEM] + [HBM] * len(fetched),
        out_specs=[VMEM] * 4,
        out_shape=[jax.ShapeDtypeStruct((rows, inner), BF16), wide, wide, wide],
        scratch_shapes=[pltpu.VMEM(array.shape, BF16) for array in fetched]
        + [pltpu.SemaphoreType.DMA((13,))],
        compiler_params=pltpu.CompilerParams(vmem_limit_bytes=24 * MIB),
        cost_estimate=pl.CostEstimate(flops=1, bytes_accessed=1, transcendentals=0),
        name="first_part",
    )(embeds, *in_hbm(*fetched))


def weigh_kernel(q_ref, acc_ref, top_ref, total_ref, key_ref, embed_ref, keep_ref, inverse_ref, weight_ref):
    half = key_ref.shape[0]
    for head in range(HEADS):
        at = columns(head)
        key = (key_ref[:, at].astype(F32) + embed_ref[1:2, at]).astype(BF16)
        for block in range(q_ref.shape[0] // half):
            here = slice(block * half, (block + 1) * half)
            scores = dot_nt(q_ref[here, at], key)
            before = top_ref[here, at]
            top = jnp.maximum(before, jnp.max(scores, axis=-1, keepdims=True))
            keep = jnp.exp2((before - top) * EXP2_SCALE)
            expo = jnp.exp2((scores - jnp.concatenate([top, top], axis=1)) * EXP2_SCALE).astype(BF16)
            weight_ref[here, head * half : (head + 1) * half] = expo
            total = dot_f32(expo, jnp.ones((half, HEAD_DIM), BF16)) + total_ref[here, at] * keep
            inverse_ref[here, at] = 1.0 / total
            keep_ref[here, at] = acc_ref[here, at] * keep


def weigh(query, acc, top, total, key, embeds):
    rows, inner = query.shape
    wide = jax.ShapeDtypeStruct((rows, inner), F32)
    return pl.pallas_call(
        weigh_kernel,
        in_specs=[VMEM] * 6,
        out_specs=[VMEM] * 3,
        out_shape=[wide, wide, jax.ShapeDtypeStruct((rows, HEADS * key.shape[0]), BF16)],
        compiler_params=pltpu.CompilerParams(vmem_limit_bytes=6 * MIB),
        cost_estimate=pl.CostEstimate(flops=1, bytes_accessed=1, transcendentals=0),
        name="weigh",
    )(query, acc, top, total, key, embeds)


def last_kernel(acc_ref, inverse_ref, weight_ref, piece_a_ref, piece_b_ref, stream_a_ref, stream_b_ref, w_ref, o_hbm, out_ref, o_ref, sems):
    rows = stream_a_ref.shape[0]
    keys = piece_a_ref.shape[0]
    inner = HEADS * HEAD_DIM
    copies = []
    for block, stream_ref in enumerate((stream_a_ref, stream_b_ref)):
        here = slice(block * rows, (block + 1) * rows)
        for head in range(HEADS):
            at = columns(head)
            weights = weight_ref[here, head * keys : (head + 1) * keys]
            first = inner + head * HEAD_DIM
            value_at = slice(first, first + HEAD_DIM)
            value = alone_part((piece_a_ref, piece_b_ref), value_at, FIRST_PIECE)[...]
            acc = acc_ref[here, at] + dot_f32(weights, value)
            out_ref[here, at] = (acc * inverse_ref[here, at]).astype(BF16)
        for i in range(4):
            cols = slice(i * 512, (i + 1) * 512)
            product = dot_f32(out_ref[here, :], w_ref[:, cols])
            o_ref[here, cols] = (stream_ref[:, cols].astype(F32) + product).astype(BF16)
            copies.append(
                pltpu.make_async_copy(
                    o_ref.at[here, cols], o_hbm.at[here, cols], sems.at[len(copies)]
                )
            )
            copies[-1].start()
    for copy in copies:
        copy.wait()


def last_part(acc, inverse, weights, pieces, streams, w_out):
    inner, width = w_out.shape
    rows = acc.shape[0]
    return pl.pallas_call(
        last_kernel,
        in_specs=[VMEM] * 8,
        out_specs=HBM,
        out_shape=pltpu.HBM((rows, width), BF16),
        scratch_shapes=[
            pltpu.VMEM((rows, inner), BF16),
            pltpu.VMEM((rows, width), BF16),
            pltpu.SemaphoreType.DMA((8,)),
        ],
        compiler_params=pltpu.CompilerParams(vmem_limit_bytes=8 * MIB),
        cost_estimate=pl.CostEstimate(flops=1, bytes_accessed=1, transcendentals=0),
        name="last_part",
    )(acc, inverse, weights, *pieces, *streams, w_out)


def shards(
    hidden,
    t_query,
    t_key,
    t_value,
    frame_offsets,
    cycle_sides,
    w_temporal_out,
    norm_gain,
    w_query,
    w_key,
    w_value,
    w_cross_out,
    side_embed,
):
    rows_here = hidden.shape[2]
    model_width = hidden.shape[3]
    inner = t_query.shape[3]
    frames = lax.axis_size("frame")
    half = rows_here // 2
    group = half // frames
    hidden = hidden.reshape(rows_here, model_width)
    t_query = t_query.reshape(rows_here, inner)
    t_key = t_key.reshape(rows_here, inner)
    t_value = t_value.reshape(rows_here, inner)
    gain = norm_gain
    offsets = jnp.broadcast_to(frame_offsets.astype(F32)[:, None], (frames, HEAD_DIM))

    def exchange(value):
        return lax.all_to_all(value, "frame", split_axis=0, concat_axis=0, tiled=True)

    def to_near(value):
        return lax.ppermute(value, "cam", [(0, 1), (1, 0), (2, 3), (3, 2)])

    def to_far(value):
        return lax.ppermute(value, "cam", [(0, 3), (3, 0), (1, 2), (2, 1)])

    packed_a, cosine, sine = pack(t_query, t_key, t_value, offsets, rotary_frequencies())
    got_a = exchange(packed_a)
    weights = (w_temporal_out, gain, w_key, w_value)
    got_b = exchange(temporal(got_a, cosine, sine, group, [t_query, t_key, t_value]))
    stream_a, normed_a, kv_a, key_a, value_a = project_first(got_b, 3 * inner, hidden, *weights)
    far_key_a = to_far(key_a)
    far_key_a, value_a = lax.optimization_barrier((far_key_a, value_a))
    far_value_a = to_far(value_a)
    near_a = to_near(kv_a)
    got_b, key_a = lax.optimization_barrier((got_b, key_a))
    back_b = exchange(temporal(got_b, cosine, sine, group, []))
    stream_b, normed_b, kv_b, piece_b, rest_b = project_second(back_b, hidden, *weights)
    far_piece_b = to_far(piece_b)
    far_rest_b = to_far(rest_b)
    near_b = to_near(kv_b)
    token = side_embed[:, :HEAD_DIM]
    far_value_a, token = lax.optimization_barrier((far_value_a, token))
    token = to_near(token)
    token = to_near(token + 1)
    stream_b, cycle_sides, side_embed = lax.optimization_barrier((stream_b, cycle_sides, side_embed))
    near_cam = lax.axis_index("cam") ^ 1
    near_left = cycle_sides[0, 0] == near_cam
    side_f = side_embed.astype(F32)
    embeds = jnp.where(near_left, side_f, side_f[::-1])
    embeds, token = lax.optimization_barrier((embeds, token))
    embeds = embeds + 0.0 * token[:1, :1].astype(F32)
    query, acc, top, total = first_part(
        [normed_a, normed_b], w_query, embeds, [kv_a, kv_b], [near_a, near_b], far_key_a, far_value_a
    )
    acc, inverse, last_weights = weigh(query, acc, top, total, far_piece_b, embeds)
    mixed = last_part(acc, inverse, last_weights, [far_piece_b, far_rest_b], [stream_a, stream_b], w_cross_out)
    return mixed.reshape(1, 1, rows_here, model_width)


def solution(mesh):
    in_specs = (
        P("cam", "frame", None, None),
        P("cam", "frame", None, None),
        P("cam", "frame", None, None),
        P("cam", "frame", None, None),
        P(),
        P("cam", None),
        P(),
        P(),
        P(),
        P(),
        P(),
        P(),
        P(),
    )
    out_specs = P("cam", "frame", None, None)
    return jax.shard_map(shards, mesh=mesh, in_specs=in_specs, out_specs=out_specs, check_vma=False)
```
